128 devices in a mesh: group: 8 (over x, y_hi), replica: 16 (over z, y_lo, core).
Axes of the slice: x: 4, y: 4 (y_hi: 2, y_lo: 2; y = y_hi * 2 + y_lo), z: 4, core: 2. Of those that a mesh axis runs over, the one named last changes fastest.
Arguments:
- tokens: bfloat16 [16, 1024, 1152], P('replica', 'group'), may hold values from -6 to 6
- positions: int32 [16, 1024], P('replica', 'group'), may hold values from 0 to 1023, as said below
- cotangent: bfloat16 [16, 1024, 1152], P('replica', 'group'), may hold values from -6 to 6
- gain_attn: float32 [1152], replicated, may hold values from 0.25 to 1.75
- gain_query: float32 [256], replicated, may hold values from 0.25 to 1.75
- gain_key: float32 [256], replicated, may hold values from 0.25 to 1.75
- gain_post_attn: float32 [1152], replicated, may hold values from 0.25 to 1.75
- gain_ffn: float32 [1152], replicated, may hold values from 0.25 to 1.75
- gain_post_ffn: float32 [1152], replicated, may hold values from 0.25 to 1.75
- w_query: bfloat16 [1152, 1024], P('group'), may hold values from -0.1875 to 0.1875
- w_key: bfloat16 [1152, 256], P('group'), may hold values from -0.1875 to 0.1875
- w_value: bfloat16 [1152, 256], P('group'), may hold values from -0.1875 to 0.1875
- w_out: bfloat16 [1152, 1024], P('group'), may hold values from -0.1875 to 0.1875
- w_gate: bfloat16 [1152, 6912], P('group'), may hold values from -0.1875 to 0.1875
- w_up: bfloat16 [1152, 6912], P('group'), may hold values from -0.1875 to 0.1875
- w_down: bfloat16 [1152, 6912], P('group'), may hold values from -0.078125 to 0.078125
Outputs:
- mixed_out: bfloat16 [16, 1024, 1152], P('replica', 'group')
- grad_tokens: float32 [16, 1024, 1152], P('replica', 'group')
- grad_gain_attn: float32 [1152], replicated
- grad_gain_query: float32 [256], replicated
- grad_gain_key: float32 [256], replicated
- grad_gain_post_attn: float32 [1152], replicated
- grad_gain_ffn: float32 [1152], replicated
- grad_gain_post_ffn: float32 [1152], replicated
- grad_query: float32 [1152, 1024], P('group')
- grad_key: float32 [1152, 256], P('group')
- grad_value: float32 [1152, 256], P('group')
- grad_out: float32 [1152, 1024], P('group')
- grad_gate: float32 [1152, 6912], P('group')
- grad_up: float32 [1152, 6912], P('group')
- grad_down: float32 [1152, 6912], P('group')
The draws below stay inside these ranges and needn't reach their ends.
Inputs may be any that keep to these rules, and one draw needn't show every extreme that they name: Within a sequence, positions rise by one from token to token inside a document and are 0 at a document's first token; the first document starts at the sequence's first token. In each block of 1 sequence one document leaves fewer than 128 tokens of its sequence before it and after it; one sequence of the first block is a single document.
All inputs are finite; a program needn't handle non-finite values.
Results may differ from the reference program's by a relative error of at most 0.025.
Values may be sent and summed in bfloat16 or wider, within the bound.
No kernel may reach another device: no remote copies, remote signals or barrier semaphores. Data moves between devices by JAX's collectives and lax.ppermute only.
A program may use at most 320 MiB of HBM per device.

```python
import jax
import jax.numpy as jnp
from jax import lax

D = 1152
HEADS = 4
HEAD = 256
FF = 6912
WINDOW = 512
LENGTH = 1024
SEQ_GRP = 1
SEQS = 16
TOK_DEV = 128


def draw_positions(key, part):
    key = jax.random.fold_in(key, 11)
    key_spread, key_first, key_last, key_chosen = jax.random.split(key, 4)
    spread_edges = jax.random.randint(key_spread, (SEQS, 3), 1, LENGTH)
    first_edge = jax.random.randint(key_first, (SEQS,), 1, TOK_DEV)
    last_edge = jax.random.randint(key_last, (SEQS,), LENGTH - TOK_DEV + 1, LENGTH)
    chosen = jax.random.randint(key_chosen, (SEQS // SEQ_GRP,), 0, SEQ_GRP)
    seq_number = jnp.arange(SEQS, dtype=jnp.int32)
    member = seq_number % SEQ_GRP == jnp.repeat(chosen, SEQ_GRP)
    whole_one = member & (seq_number < SEQ_GRP)
    reaching = jnp.stack([first_edge, last_edge, first_edge], axis=1)
    edges = jnp.where(member[:, None], reaching, spread_edges)
    edges = jnp.where(whole_one[:, None], LENGTH, edges)
    token_index = jnp.arange(LENGTH, dtype=jnp.int32)
    starts = jnp.max(jnp.where(edges[:, :, None] <= token_index[None, None, :], edges[:, :, None], 0), axis=1)
    return (token_index[None, :] - starts).astype(jnp.int32)


def level_of(key, shape, cuts, least, top_value):
    gain = 1.0
    for dim, shards_of in cuts:
        steps = jax.random.uniform(jax.random.fold_in(jax.random.fold_in(key, 6), dim), (shards_of,), jnp.float32, least / len(cuts), top_value / len(cuts))
        gain = gain * jnp.repeat(jnp.exp(steps), shape[dim] // shards_of).reshape((-1,) + (1,) * (len(shape) - 1 - dim))
    return gain


def centred(own_key, extent, deviation, reach, cuts=(), kind=jnp.bfloat16):
    drawn = deviation * jax.random.normal(own_key, extent, jnp.float32)
    if cuts:
        drawn = drawn * level_of(own_key, extent, cuts, -0.22, 0.18)
    return jnp.clip(drawn, -reach, reach).astype(kind)


def setup_inputs(seed: int = 0) -> dict:
    arg_keys = jax.random.split(jax.random.key(seed), 17)
    return {
        "tokens": centred(arg_keys[0], (SEQS, LENGTH, D), 1.0, 6.0, ((0, 16), (1, 8))),
        "positions": draw_positions(jax.random.fold_in(arg_keys[16], 71), 0),
        "cotangent": centred(arg_keys[2], (SEQS, LENGTH, D), 1.0, 6.0, ((0, 16), (1, 8))),
        "gain_attn": jnp.clip(1.0 + 0.15 * jax.random.normal(arg_keys[3], (D,), jnp.float32), 0.25, 1.75),
        "gain_query": jnp.clip(1.0 + 0.15 * jax.random.normal(arg_keys[4], (HEAD,), jnp.float32), 0.25, 1.75),
        "gain_key": jnp.clip(1.0 + 0.15 * jax.random.normal(arg_keys[5], (HEAD,), jnp.float32), 0.25, 1.75),
        "gain_post_attn": jnp.clip(1.0 + 0.15 * jax.random.normal(arg_keys[6], (D,), jnp.float32), 0.25, 1.75),
        "gain_ffn": jnp.clip(1.0 + 0.15 * jax.random.normal(arg_keys[7], (D,), jnp.float32), 0.25, 1.75),
        "gain_post_ffn": jnp.clip(1.0 + 0.15 * jax.random.normal(arg_keys[8], (D,), jnp.float32), 0.25, 1.75),
        "w_query": centred(arg_keys[9], (D, HEADS * HEAD), D ** -0.5, 0.1875, ((0, 8),)),
        "w_key": centred(arg_keys[10], (D, HEAD), D ** -0.5, 0.1875, ((0, 8),)),
        "w_value": centred(arg_keys[11], (D, HEAD), D ** -0.5, 0.1875, ((0, 8),)),
        "w_out": centred(arg_keys[12], (D, HEADS * HEAD), (HEADS * HEAD) ** -0.5, 0.1875, ((0, 8),)),
        "w_gate": centred(arg_keys[13], (D, FF), D ** -0.5, 0.1875, ((0, 8),)),
        "w_up": centred(arg_keys[14], (D, FF), D ** -0.5, 0.1875, ((0, 8),)),
        "w_down": centred(arg_keys[15], (D, FF), FF ** -0.5, 0.078125, ((0, 8),)),
    }


@jax.custom_vjp
def low(v):
    return lax.optimization_barrier(v.astype(jnp.bfloat16)).astype(jnp.float32)

@jax.custom_vjp
def low_back(v):
    return v

def low_keep(v):
    return (low(v), None)

def low_pass(kept, grad):
    return (grad,)

def back_keep(v):
    return (v, None)

def back_low(kept, grad):
    return (low(grad),)
low.defvjp(low_keep, low_pass)
low_back.defvjp(back_keep, back_low)
EPSILON = 1e-06
ROPE_BASE = 10000.0
MASKED = -1e+30
HIGHEST = lax.Precision.HIGHEST

def norm_rows(entries, gain_row):
    return entries * lax.rsqrt(lax.optimization_barrier(jnp.mean(entries * entries, axis=-1, keepdims=True)) + EPSILON) * gain_row

def turn_tables(position_row, head_width):
    half_width = head_width // 2
    frequency = ROPE_BASE ** (-2.0 * jnp.arange(half_width, dtype=jnp.float32) / head_width)
    angles = position_row.astype(jnp.float32)[..., None] * frequency
    return (jnp.cos(angles), jnp.sin(angles))

def rotate(entries, cosine_table, sine_table):
    half_width = entries.shape[-1] // 2
    leading = entries[..., :half_width]
    trailing = entries[..., half_width:]
    return jnp.concatenate([leading * cosine_table - trailing * sine_table, trailing * cosine_table + leading * sine_table], axis=-1)

def matmul_high(left_side, right_side):
    return jnp.dot(left_side, right_side, precision=HIGHEST)

def whole_layer(sequence, position_row, params):
    gain_attn, gain_query, gain_key, gain_post_attn, gain_ffn, gain_post_ffn, w_query, w_key, w_value, w_out, w_gate, w_up, w_down = params
    cosine_table, sine_table = turn_tables(position_row, HEAD)
    normed = low(norm_rows(sequence, gain_attn))
    query_raw = low_back(matmul_high(normed, w_query)).reshape(LENGTH, HEADS, HEAD)
    key_raw = low_back(matmul_high(normed, w_key))
    value_raw = low_back(matmul_high(normed, w_value))
    queries = low(rotate(norm_rows(query_raw, gain_query), cosine_table[:, None, :], sine_table[:, None, :]) * HEAD ** (-0.5))
    key_rows = low(rotate(norm_rows(key_raw, gain_key), cosine_table, sine_table))
    value_rows = low(value_raw)
    token_index = jnp.arange(LENGTH, dtype=jnp.int32)
    distance = token_index[:, None] - token_index[None, :]
    allowed = (distance >= 0) & (distance < WINDOW) & (position_row[:, None] - position_row[None, :] == distance)
    scores = low_back(jnp.einsum('qhd,kd->hqk', queries, key_rows, precision=HIGHEST))
    scores = jnp.where(allowed[None], scores, MASKED)
    probabilities = jax.nn.softmax(scores, axis=-1)
    mixed_heads = low(low_back(jnp.einsum('hqk,kd->qhd', low(probabilities), value_rows, precision=HIGHEST)))
    attended = mixed_heads.reshape(LENGTH, HEADS * HEAD)
    attn_branch = low_back(matmul_high(attended, w_out.T))
    middle = sequence + norm_rows(attn_branch, gain_post_attn)
    normed_ffn = low(norm_rows(middle, gain_ffn))
    gate_proj = low_back(matmul_high(normed_ffn, w_gate))
    up_proj = low_back(matmul_high(normed_ffn, w_up))
    hidden = low(jax.nn.gelu(gate_proj, approximate=True) * up_proj)
    ffn_branch = low_back(matmul_high(hidden, w_down.T))
    return middle + norm_rows(ffn_branch, gain_post_ffn)

def reference(tokens, positions, cotangent, gain_attn, gain_query, gain_key, gain_post_attn, gain_ffn, gain_post_ffn, w_query, w_key, w_value, w_out, w_gate, w_up, w_down):
    params = tuple((member.astype(jnp.float32) for member in (gain_attn, gain_query, gain_key, gain_post_attn, gain_ffn, gain_post_ffn, w_query, w_key, w_value, w_out, w_gate, w_up, w_down)))

    def run_layer(inputs, weights_all):

        def one_sequence(paired):
            sequence, position_row = paired

            def layer_here(sequence_in, weights_in):
                return whole_layer(sequence_in, position_row, weights_in)
            return jax.checkpoint(layer_here)(sequence, weights_all)
        return lax.map(one_sequence, (inputs, positions))
    outputs, pullback = jax.vjp(run_layer, tokens.astype(jnp.float32), params)
    grad_tokens, grad_params = pullback(cotangent.astype(jnp.float32))
    return (outputs.astype(jnp.bfloat16), grad_tokens, grad_params[0], grad_params[1], grad_params[2], grad_params[3], grad_params[4], grad_params[5], grad_params[6], grad_params[7], grad_params[8], grad_params[9], grad_params[10], grad_params[11], grad_params[12])
```

```python
import jax
import jax.numpy as jnp
from jax import lax
from jax.experimental import pallas as pl
from jax.experimental.pallas import tpu as pltpu
from jax.sharding import Mesh
from jax.sharding import PartitionSpec as P

HEADS = 4
WINDOW = 512


EPSILON = 1e-06
ROPE_BASE = 10000.0
MASKED = -1e30
CONTRACT_COLS = (((1,), (1,)), ((), ()))
CONTRACT_ROWS = (((0,), (0,)), ((), ()))


GROUP = ("x", "yh")
REPLICA = ("z", "yl", "core")
SHIFTS = ((1, 0), (3, 0), (0, 1), (1, 1), (3, 1), (2, 0), (2, 1))
Z_STEPS = (1, 3, 2)
LANES = 128
UNIT_TILES = 7


def from_behind(block, distance):
    devices = range(8)
    route = [(i - distance, i) for i in devices if i - distance in devices]
    return lax.ppermute(block, GROUP, route)


def shifted(block, step):
    route = [(a * 2 + b, (a + step[0]) % 4 * 2 + (b ^ step[1])) for a in range(4) for b in range(2)]
    return lax.ppermute(block, GROUP, route)


def turned(block, axis, step, size):
    return lax.ppermute(block, axis, [(i, (i + step) % size) for i in range(size)])


def swapped(block, axis):
    return turned(block, axis, 1, 2)


def pick(stack, index):
    return lax.dynamic_index_in_dim(stack, index, 0, keepdims=False)


def place(stack, block, index):
    return lax.dynamic_update_index_in_dim(stack, block, index, 0)


def group_index(step=(0, 0), sign=1):
    along_x = lax.rem(lax.axis_index("x") + 4 + sign * step[0], 4)
    return along_x * 2 + (lax.axis_index("yh") ^ step[1])


def gather_rows(shard):
    stack = place(jnp.zeros((8,) + shard.shape, shard.dtype), shard, group_index())
    for step in SHIFTS:
        stack = place(stack, shifted(shard, step), group_index(step, -1))
    return stack.reshape((-1,) + shard.shape[1:])


def by_core(first, second):
    held = jnp.where(lax.axis_index("core") == 0, first, second)
    return held


def core_pair(held):
    other = swapped(held, "core")
    is_first = lax.axis_index("core") == 0
    return jnp.where(is_first, held, other), jnp.where(is_first, other, held)


def gather_tokens(rows):
    return jnp.concatenate([rows] + [shifted(rows, step) for step in SHIFTS], axis=0)


def scatter_tokens(partial):
    rows = partial.shape[0] // 8
    total = partial[:rows]
    for i, step in enumerate(SHIFTS):
        back = ((4 - step[0]) % 4, step[1])
        block = partial[(i + 1) * rows : (i + 2) * rows].astype(jnp.bfloat16)
        total = total + shifted(block, back).astype(jnp.float32)
    return total


def piece_table():
    depth, core = lax.axis_index("z"), lax.axis_index("core")
    along = [lax.rem(depth + 4 - step, 4) for step in (0,) + Z_STEPS]
    return jnp.stack([(core if own else 1 - core) * 4 + z for own in (True, False) for z in along])


def source_table():
    return jnp.stack([group_index(step, -1) for step in ((0, 0),) + SHIFTS])


def unit_kernel(piece_ref, gate_ref, up_ref, down_ref, out_ref):
    piece = piece_ref[0]
    real = (piece < UNIT_TILES) & (pl.program_id(0) * UNIT_TILES + piece < piece_ref[1])
    for i, ref in enumerate((gate_ref, up_ref, down_ref)):
        block = ref[...]
        out_ref[0, :, i * LANES : (i + 1) * LANES] = jnp.where(real, block, jnp.zeros_like(block))


def unit_pieces(w_gate, w_up, w_down):
    rows, units = w_gate.shape
    tiles = units // LANES
    piece = lax.axis_index("core") * 4 + lax.axis_index("z")
    numbers = jnp.stack([piece, jnp.int32(tiles)])
    spec = pl.BlockSpec(
        (rows, LANES), lambda j, num: (0, jnp.minimum(j * UNIT_TILES + num[0], tiles - 1))
    )
    return pl.pallas_call(
        unit_kernel,
        out_shape=jax.ShapeDtypeStruct((8, rows, 3 * LANES), jnp.bfloat16),
        grid_spec=pltpu.PrefetchScalarGridSpec(
            num_scalar_prefetch=1,
            grid=(8,),
            in_specs=[spec] * 3,
            out_specs=pl.BlockSpec((1, rows, 3 * LANES), lambda j, num: (j, 0, 0)),
        ),
    )(numbers, w_gate, w_up, w_down)


def unit_shards(pieces):
    me = group_index()
    stack = place(jnp.zeros_like(pieces), pick(pieces, me), me)
    for step in SHIFTS:
        block = shifted(pick(pieces, group_index(step)), step)
        stack = place(stack, block, group_index(step, -1))
    stack = stack.reshape(-1, 3 * LANES)
    mine = [stack] + [turned(stack, "z", step, 4) for step in Z_STEPS]
    other = swapped(jnp.stack(mine), "core")
    slots = mine + [other[i] for i in range(4)]
    return tuple(
        jnp.concatenate([slot[:, i * LANES : (i + 1) * LANES] for slot in slots], axis=1)
        for i in range(3)
    )


def plus(*blocks):
    return sum(block.astype(jnp.float32) for block in blocks).astype(jnp.bfloat16)


def assemble_units_kernel(table_ref, mine_ref, other_ref, *out_refs):
    for slot in range(8):
        held = mine_ref if slot < 4 else other_ref
        piece = table_ref[slot]

        @pl.when(piece < UNIT_TILES)
        def _():
            cols = pl.ds(pl.multiple_of(piece * LANES, LANES), LANES)
            for i, out_ref in enumerate(out_refs):
                block = held[slot % 4, 0, :, i * LANES : (i + 1) * LANES]
                out_ref[:, cols] = block.astype(jnp.float32)


def assemble_units(mine, other, units):
    rows = mine.shape[2]
    table = jnp.concatenate([piece_table(), source_table()])
    block = UNIT_TILES * LANES
    spec = pl.BlockSpec((4, 1, rows, 3 * LANES), lambda r, table: (0, r, 0, 0))
    return pl.pallas_call(
        assemble_units_kernel,
        out_shape=[jax.ShapeDtypeStruct((rows, units), jnp.float32)] * 3,
        grid_spec=pltpu.PrefetchScalarGridSpec(
            num_scalar_prefetch=1,
            grid=(8,),
            in_specs=[spec] * 2,
            out_specs=[pl.BlockSpec((rows, block), lambda r, table: (0, table[8 + r]))] * 3,
        ),
        compiler_params=pltpu.CompilerParams(vmem_limit_bytes=32 * 2**20),
    )(table, mine, other)


def assemble_attn_kernel(table_ref, mine_ref, other_ref, query_ref, out_ref, pair_ref):
    for slot in range(8):
        held = mine_ref if slot < 4 else other_ref
        piece = table_ref[slot]
        cols = pl.ds(pl.multiple_of(piece * LANES, LANES), LANES)
        block = held[slot % 4].astype(jnp.float32)
        query_ref[:, cols] = block[:, :LANES]
        out_ref[:, cols] = block[:, LANES : 2 * LANES]

        @pl.when(piece < 4)
        def _():
            pair_ref[:, cols] = block[:, 2 * LANES :]


def assemble_attn(mine, other):
    rows = mine.shape[1]
    return pl.pallas_call(
        assemble_attn_kernel,
        out_shape=[
            jax.ShapeDtypeStruct((rows, width * LANES), jnp.float32) for width in (8, 8, 4)
        ],
        in_specs=[pl.BlockSpec(memory_space=pltpu.SMEM)]
        + [pl.BlockSpec(memory_space=pltpu.VMEM)] * 2,
        out_specs=[pl.BlockSpec(memory_space=pltpu.VMEM)] * 3,
        compiler_params=pltpu.CompilerParams(vmem_limit_bytes=32 * 2**20),
    )(piece_table(), mine, other)


def to_slots(grad):
    return jnp.transpose(grad.reshape(grad.shape[0], -1, LANES), (1, 0, 2))


def unit_grads(grad_gate, grad_up, grad_down, units):
    slots = jnp.concatenate([to_slots(g) for g in (grad_gate, grad_up, grad_down)], axis=2)
    mine, other = slots[:4], slots[4:]
    total = plus(mine, swapped(other, "core"))
    total = plus(
        total[0],
        *[turned(total[1 + i], "z", (4 - step) % 4, 4) for i, step in enumerate(Z_STEPS)],
    )
    total = total.reshape(8, 144, 3 * LANES)
    blocks = [pick(total, group_index())]
    blocks += [shifted(pick(total, group_index(step)), step) for step in SHIFTS]
    stack = jnp.stack(blocks)
    stack = plus(stack, swapped(stack, "yl"))
    mine = jnp.stack([stack] + [turned(stack, "z", step, 4) for step in Z_STEPS])
    return assemble_units(mine, swapped(mine, "core"), units)


def attn_grads_of(grad_projected, grad_out):
    query, pair = grad_projected[:, :1024], grad_projected[:, 1024:]
    pair = jnp.pad(pair, ((0, 0), (0, 512)))
    slots = jnp.concatenate([to_slots(g) for g in (query, grad_out, pair)], axis=2)
    core, depth = lax.axis_index("core"), lax.axis_index("z")
    halves = slots.reshape((2, 4) + slots.shape[1:])
    total = plus(pick(halves, core), swapped(pick(halves, 1 - core), "core"))
    total = plus(
        pick(total, depth),
        *[turned(pick(total, lax.rem(depth + step, 4)), "z", step, 4) for step in Z_STEPS],
    )
    total = total.reshape(8, 144, 3 * LANES)
    total = plus(
        pick(total, group_index()),
        *[shifted(pick(total, group_index(step)), step) for step in SHIFTS],
    )
    total = plus(total, swapped(total, "yl"))
    mine = jnp.stack([total] + [turned(total, "z", step, 4) for step in Z_STEPS])
    return assemble_attn(mine, swapped(mine, "core"))


def total_vector(vector):
    for axis in ("core", "yl", "yh"):
        vector = vector + swapped(vector, axis)
    for axis in ("z", "x"):
        for flip in (1, 2):
            vector = vector + lax.ppermute(vector, axis, [(i, i ^ flip) for i in range(4)])
    return vector


def norm_rows(entries, gain_row):
    return (
        entries
        * lax.rsqrt(jnp.mean(entries * entries, axis=-1, keepdims=True) + EPSILON)
        * gain_row
    )


def turn_tables(position_rows, head_width):
    half_width = head_width // 2
    frequency = ROPE_BASE ** (-2.0 * jnp.arange(half_width, dtype=jnp.float32) / head_width)
    angles = position_rows.astype(jnp.float32)[..., None] * frequency
    return (jnp.cos(angles), jnp.sin(angles))


def rotate(entries, cosine_table, sine_table):
    half_width = entries.shape[-1] // 2
    leading = entries[..., :half_width]
    trailing = entries[..., half_width:]
    return jnp.concatenate(
        [
            leading * cosine_table - trailing * sine_table,
            trailing * cosine_table + leading * sine_table,
        ],
        axis=-1,
    )


def query_piece(raw_proj, gain_row, cosine_table, sine_table):
    head_width = gain_row.shape[0]
    shaped = raw_proj.reshape(cosine_table.shape[0], cosine_table.shape[1], -1, head_width)
    turned = rotate(
        norm_rows(shaped, gain_row), cosine_table[:, :, None, :], sine_table[:, :, None, :]
    )
    return jnp.transpose(turned, (0, 2, 1, 3)) * head_width ** (-0.5)


def key_piece(raw_proj, gain_row, cosine_table, sine_table):
    shaped = raw_proj.reshape(cosine_table.shape[0], cosine_table.shape[1], gain_row.shape[0])
    return rotate(norm_rows(shaped, gain_row), cosine_table, sine_table)


def gelu_product(gate_proj, up_proj):
    return jax.nn.gelu(gate_proj, approximate=True) * up_proj


def masked_scores(queries, key_rows, allowed):
    plain = jnp.einsum("shqd,skd->shqk", queries, key_rows, preferred_element_type=jnp.float32)
    return jnp.where(allowed, plain, MASKED)


def transposed_product(left_side, right_side):
    return lax.dot_general(left_side, right_side, CONTRACT_ROWS, preferred_element_type=jnp.float32)


def product_by_rows(left_side, right_side):
    return lax.dot_general(left_side, right_side, CONTRACT_COLS, preferred_element_type=jnp.float32)


def local(
    tokens,
    positions,
    cotangent,
    gain_attn,
    gain_query,
    gain_key,
    gain_post_attn,
    gain_ffn,
    gain_post_ffn,
    w_query,
    w_key,
    w_value,
    w_out,
    w_gate,
    w_up,
    w_down,
):
    seq_count, tok_rows, model_width = tokens.shape
    all_rows = seq_count * tok_rows
    head_width = gain_query.shape[0]
    query_cols = w_query.shape[1]
    reach_back = min(-(-(WINDOW - 1) // tok_rows), 7)
    cosine_table, sine_table = turn_tables(positions, head_width)
    inputs = tokens.astype(jnp.float32).reshape(all_rows, model_width)
    normed_full, norm_attn_back = jax.vjp(norm_rows, inputs, gain_attn)
    normed = normed_full.astype(jnp.bfloat16)
    qkv_held = by_core(
        w_query[:, :768], jnp.concatenate([w_query[:, 768:], w_key, w_value], axis=1)
    )
    qkv_rows = lax.all_to_all(jnp.broadcast_to(qkv_held, (8,) + qkv_held.shape), GROUP, 0, 0)
    unit_held = unit_pieces(w_gate, w_up, w_down)
    qkv_first, qkv_second = core_pair(qkv_rows.reshape(model_width, -1))
    out_held = by_core(w_out[:, :512], w_out[:, 512:])
    out_held, unit_held, _ = lax.optimization_barrier((out_held, unit_held, qkv_rows))
    out_rows = gather_rows(out_held)
    out_first, out_second = core_pair(out_rows)
    unit_held, _ = lax.optimization_barrier((unit_held, out_rows))
    gate_cols, up_cols, down_cols = unit_shards(unit_held)
    first_raw = jnp.dot(normed, qkv_first, preferred_element_type=jnp.float32)
    second_raw = jnp.dot(normed, qkv_second, preferred_element_type=jnp.float32)
    query_raw = jnp.concatenate([first_raw, second_raw[:, :256]], axis=1)
    key_raw = second_raw[:, 256:512]
    value_raw = second_raw[:, 512:]

    def query_local(raw_proj, gain_row):
        return query_piece(raw_proj, gain_row, cosine_table, sine_table)

    def key_local(raw_proj, gain_row):
        return key_piece(raw_proj, gain_row, cosine_table, sine_table)

    queries_full, query_back = jax.vjp(query_local, query_raw, gain_query)
    keys_full, key_back = jax.vjp(key_local, key_raw, gain_key)
    queries = queries_full.astype(jnp.bfloat16)
    local_pairs = jnp.concatenate(
        [keys_full, value_raw.reshape(seq_count, tok_rows, head_width)], axis=-1
    ).astype(jnp.bfloat16)
    collected = [local_pairs]
    for distance in range(1, reach_back + 1):
        collected.insert(0, from_behind(local_pairs, distance))
    pair_rows = jnp.concatenate(collected, axis=1)
    key_rows = pair_rows[..., :head_width]
    value_rows = pair_rows[..., head_width:]
    place_index = group_index()
    query_index = place_index * tok_rows + jnp.arange(tok_rows, dtype=jnp.int32)
    key_index = (place_index - reach_back) * tok_rows + jnp.arange(
        (reach_back + 1) * tok_rows, dtype=jnp.int32
    )
    offsets = query_index[:, None] - key_index[None, :]
    doc_start = query_index[None, :] - positions
    allowed = ((offsets >= 0) & (offsets < WINDOW))[None, :, :] & (
        key_index[None, None, :] >= doc_start[:, :, None]
    )
    allowed = allowed[:, None, :, :]
    scores = masked_scores(queries, key_rows, allowed)
    highest = jnp.max(scores, axis=-1, keepdims=True)
    exp_scores = jnp.exp(scores - highest)
    sum_scores = jnp.sum(exp_scores, axis=-1, keepdims=True)
    log_total = highest + jnp.log(sum_scores)
    weights = (exp_scores / sum_scores).astype(jnp.bfloat16)
    mixed_heads = jnp.einsum(
        "shqk,skd->sqhd", weights, value_rows, preferred_element_type=jnp.float32
    )
    attended = mixed_heads.reshape(all_rows, query_cols).astype(jnp.bfloat16)
    attn_branch = product_by_rows(attended[:, :512], out_first) + product_by_rows(
        attended[:, 512:], out_second
    )
    attn_normed, norm_post_attn_back = jax.vjp(norm_rows, attn_branch, gain_post_attn)
    middle = inputs + attn_normed
    ffn_in_full, norm_ffn_back = jax.vjp(norm_rows, middle, gain_ffn)
    normed_ffn = ffn_in_full.astype(jnp.bfloat16)
    ffn_rows = gather_tokens(normed_ffn)
    gate_proj = jnp.dot(ffn_rows, gate_cols, preferred_element_type=jnp.float32)
    up_proj = jnp.dot(ffn_rows, up_cols, preferred_element_type=jnp.float32)
    hidden_full, gelu_back = jax.vjp(gelu_product, gate_proj, up_proj)
    hidden = hidden_full.astype(jnp.bfloat16)
    ffn_branch = scatter_tokens(product_by_rows(hidden, down_cols))
    ffn_normed, norm_post_ffn_back = jax.vjp(norm_rows, ffn_branch, gain_post_ffn)
    outputs = (middle + ffn_normed).astype(jnp.bfloat16).reshape(seq_count, tok_rows, model_width)
    upstream = cotangent.astype(jnp.float32).reshape(all_rows, model_width)
    grad_ffn_branch, grad_post_ffn = norm_post_ffn_back(upstream)
    grad_ffn_branch = grad_ffn_branch.astype(jnp.bfloat16)
    grad_branch_rows = gather_tokens(grad_ffn_branch)
    grad_hidden = jnp.dot(grad_branch_rows, down_cols, preferred_element_type=jnp.float32)
    grad_gate_full, grad_up_full = gelu_back(grad_hidden)
    grad_gate_part = grad_gate_full.astype(jnp.bfloat16)
    grad_up_part = grad_up_full.astype(jnp.bfloat16)
    grad_normed_ffn = scatter_tokens(
        product_by_rows(grad_gate_part, gate_cols) + product_by_rows(grad_up_part, up_cols)
    )
    grad_gate_total, grad_up_total, grad_down_total = unit_grads(
        transposed_product(ffn_rows, grad_gate_part).astype(jnp.bfloat16),
        transposed_product(ffn_rows, grad_up_part).astype(jnp.bfloat16),
        transposed_product(grad_branch_rows, hidden).astype(jnp.bfloat16),
        w_gate.shape[1],
    )
    grad_middle_part, grad_gain_ffn = norm_ffn_back(grad_normed_ffn)
    grad_middle = upstream + grad_middle_part
    grad_attn_branch, grad_post_attn = norm_post_attn_back(grad_middle)
    grad_attn_branch = grad_attn_branch.astype(jnp.bfloat16)
    grad_attended = jnp.concatenate(
        [
            jnp.dot(grad_attn_branch, out_first, preferred_element_type=jnp.float32),
            jnp.dot(grad_attn_branch, out_second, preferred_element_type=jnp.float32),
        ],
        axis=1,
    )
    grad_heads = grad_attended.astype(jnp.bfloat16).reshape(seq_count, tok_rows, HEADS, head_width)
    scores = masked_scores(queries, key_rows, allowed)
    probabilities = jnp.exp(scores - log_total)
    grad_probs = jnp.einsum(
        "sqhd,skd->shqk", grad_heads, value_rows, preferred_element_type=jnp.float32
    )
    centre = jnp.sum(probabilities * grad_probs, axis=-1, keepdims=True)
    grad_scores = (probabilities * (grad_probs - centre)).astype(jnp.bfloat16)
    grad_queries = jnp.einsum(
        "shqk,skd->shqd", grad_scores, key_rows, preferred_element_type=jnp.float32
    )
    grad_key_rows = jnp.einsum(
        "shqk,shqd->skd", grad_scores, queries, preferred_element_type=jnp.float32
    )
    grad_value_rows = jnp.einsum(
        "shqk,sqhd->skd",
        probabilities.astype(jnp.bfloat16),
        grad_heads,
        preferred_element_type=jnp.float32,
    )
    grad_pairs = jnp.concatenate([grad_key_rows, grad_value_rows], axis=-1)
    own_pairs = grad_pairs[:, reach_back * tok_rows :]
    for distance in range(1, reach_back + 1):
        lower_block = reach_back - distance
        sent_block = grad_pairs[:, lower_block * tok_rows : (lower_block + 1) * tok_rows]
        own_pairs = own_pairs + from_behind(
            sent_block.astype(jnp.bfloat16), -distance
        ).astype(sent_block.dtype)
    grad_key_raw, grad_gain_key = key_back(own_pairs[..., :head_width])
    grad_query_raw, grad_gain_query = query_back(grad_queries)
    grad_value_raw = own_pairs[..., head_width:].reshape(all_rows, head_width)
    grad_projected = jnp.concatenate([grad_query_raw, grad_key_raw, grad_value_raw], axis=1).astype(
        jnp.bfloat16
    )
    contribution = product_by_rows(grad_projected[:, :768], qkv_first) + product_by_rows(
        grad_projected[:, 768:], qkv_second
    )
    query_total, grad_out_total, pair_total = attn_grads_of(
        transposed_product(normed, grad_projected).astype(jnp.bfloat16),
        transposed_product(grad_attn_branch, attended).astype(jnp.bfloat16),
    )
    grad_inputs_part, grad_gain_attn = norm_attn_back(contribution)
    grad_tokens = (grad_middle + grad_inputs_part).reshape(seq_count, tok_rows, model_width)
    gains = total_vector(
        jnp.concatenate(
            [
                grad_gain_attn,
                grad_gain_query,
                grad_gain_key,
                grad_post_attn,
                grad_gain_ffn,
                grad_post_ffn,
            ]
        )
    )
    query_at, key_at = model_width, model_width + head_width
    wide_at = key_at + head_width
    return (
        outputs,
        grad_tokens,
        gains[:query_at],
        gains[query_at:key_at],
        gains[key_at:wide_at],
        gains[wide_at : wide_at + model_width],
        gains[wide_at + model_width : wide_at + 2 * model_width],
        gains[wide_at + 2 * model_width :],
        query_total,
        pair_total[:, :head_width],
        pair_total[:, head_width:],
        grad_out_total,
        grad_gate_total,
        grad_up_total,
        grad_down_total,
    )


def solution(mesh):
    fine = Mesh(mesh.devices.reshape(4, 2, 4, 2, 2), GROUP + REPLICA)
    placed = (
        P(REPLICA, GROUP, None),
        P(REPLICA, GROUP),
        P(REPLICA, GROUP, None),
        P(),
        P(),
        P(),
        P(),
        P(),
        P(),
        P(GROUP, None),
        P(GROUP, None),
        P(GROUP, None),
        P(GROUP, None),
        P(GROUP, None),
        P(GROUP, None),
        P(GROUP, None),
    )
    return jax.shard_map(
        local,
        mesh=fine,
        in_specs=placed,
        out_specs=(
            P(REPLICA, GROUP, None),
            P(REPLICA, GROUP, None),
            P(),
            P(),
            P(),
            P(),
            P(),
            P(),
            P(GROUP, None),
            P(GROUP, None),
            P(GROUP, None),
            P(GROUP, None),
            P(GROUP, None),
            P(GROUP, None),
            P(GROUP, None),
        ),
        check_vma=False,
    )
```

```python
import jax
import jax.numpy as jnp
from jax import lax
from jax.experimental import pallas as pl
from jax.experimental.pallas import tpu as pltpu
from jax.sharding import Mesh
from jax.sharding import PartitionSpec as P

HEADS = 4
WINDOW = 512


EPSILON = 1e-06
ROPE_BASE = 10000.0
MASKED = -1e30
CONTRACT_COLS = (((1,), (1,)), ((), ()))
CONTRACT_ROWS = (((0,), (0,)), ((), ()))


GROUP = ("x", "yh")
REPLICA = ("z", "yl", "core")
SHIFTS = ((1, 0), (3, 0), (0, 1), (1, 1), (3, 1), (2, 0), (2, 1))
LANES = 128
UNIT_TILES = 7


def from_behind(block, distance):
    devices = range(8)
    route = [(i - distance, i) for i in devices if i - distance in devices]
    return lax.ppermute(block, GROUP, route)


def shifted(block, step):
    route = [(a * 2 + b, (a + step[0]) % 4 * 2 + (b ^ step[1])) for a in range(4) for b in range(2)]
    return lax.ppermute(block, GROUP, route)


def turned(block, axis, step, size):
    return lax.ppermute(block, axis, [(i, (i + step) % size) for i in range(size)])


def swapped(block, axis):
    return turned(block, axis, 1, 2)


def pick(stack, index):
    return lax.dynamic_index_in_dim(stack, index, 0, keepdims=False)


def group_index():
    return lax.axis_index("x") * 2 + lax.axis_index("yh")


def exchanged(stack, axes):
    return lax.all_to_all(stack, axes, 0, 0)


def gathered(block, axes, size):
    return exchanged(jnp.broadcast_to(block, (size,) + block.shape), axes)


def on_first_core():
    return lax.axis_index("core") == 0


def by_core(first, second):
    return jnp.where(on_first_core(), first, second)


def both_cores(mine, other):
    return by_core(mine, other), by_core(other, mine)


def gather_tokens(rows):
    return jnp.concatenate([rows] + [shifted(rows, step) for step in SHIFTS], axis=0)


def scatter_tokens(partial):
    rows = partial.shape[0] // 8
    total = partial[:rows]
    for i, step in enumerate(SHIFTS):
        back = ((4 - step[0]) % 4, step[1])
        block = partial[(i + 1) * rows : (i + 2) * rows].astype(jnp.bfloat16)
        total = total + shifted(block, back).astype(jnp.float32)
    return total


def piece_table():
    core = lax.axis_index("core")
    return jnp.stack([(core if own else 1 - core) * 4 + z for own in (True, False) for z in range(4)])


def unit_kernel(piece_ref, gate_ref, up_ref, down_ref, out_ref):
    piece = piece_ref[0]
    real = (piece < UNIT_TILES) & (pl.program_id(0) * UNIT_TILES + piece < piece_ref[1])
    for i, ref in enumerate((gate_ref, up_ref, down_ref)):
        block = ref[...]
        out_ref[0, :, i * LANES : (i + 1) * LANES] = jnp.where(real, block, jnp.zeros_like(block))


def unit_pieces(w_gate, w_up, w_down):
    rows, units = w_gate.shape
    tiles = units // LANES
    piece = lax.axis_index("core") * 4 + lax.axis_index("z")
    numbers = jnp.stack([piece, jnp.int32(tiles)])
    spec = pl.BlockSpec(
        (rows, LANES), lambda j, num: (0, jnp.minimum(j * UNIT_TILES + num[0], tiles - 1))
    )
    return pl.pallas_call(
        unit_kernel,
        out_shape=jax.ShapeDtypeStruct((8, rows, 3 * LANES), jnp.bfloat16),
        grid_spec=pltpu.PrefetchScalarGridSpec(
            num_scalar_prefetch=1,
            grid=(8,),
            in_specs=[spec] * 3,
            out_specs=pl.BlockSpec((1, rows, 3 * LANES), lambda j, num: (j, 0, 0)),
        ),
    )(numbers, w_gate, w_up, w_down)


def unit_shards(pieces):
    stack = exchanged(pieces, GROUP).reshape(-1, 3 * LANES)
    mine = gathered(stack, "z", 4)
    other = swapped(mine, "core")
    slots = [mine[i] for i in range(4)] + [other[i] for i in range(4)]
    return tuple(
        jnp.concatenate([slot[:, i * LANES : (i + 1) * LANES] for slot in slots], axis=1)
        for i in range(3)
    )


def plus(*blocks):
    return sum(block.astype(jnp.float32) for block in blocks).astype(jnp.bfloat16)


def summed(stack):
    return jnp.sum(stack.astype(jnp.float32), axis=0).astype(jnp.bfloat16)


def assemble_units_kernel(table_ref, mine_ref, other_ref, *out_refs):
    for slot in range(8):
        held = mine_ref if slot < 4 else other_ref
        piece = table_ref[slot]

        @pl.when(piece < UNIT_TILES)
        def _():
            cols = pl.ds(pl.multiple_of(piece * LANES, LANES), LANES)
            for i, out_ref in enumerate(out_refs):
                block = held[slot % 4, 0, :, i * LANES : (i + 1) * LANES]
                out_ref[:, cols] = block.astype(jnp.float32)


def assemble_units(mine, other, units):
    rows = mine.shape[2]
    table = piece_table()
    block = UNIT_TILES * LANES
    spec = pl.BlockSpec((4, 1, rows, 3 * LANES), lambda r, table: (0, r, 0, 0))
    return pl.pallas_call(
        assemble_units_kernel,
        out_shape=[jax.ShapeDtypeStruct((rows, units), jnp.float32)] * 3,
        grid_spec=pltpu.PrefetchScalarGridSpec(
            num_scalar_prefetch=1,
            grid=(8,),
            in_specs=[spec] * 2,
            out_specs=[pl.BlockSpec((rows, block), lambda r, table: (0, r))] * 3,
        ),
        compiler_params=pltpu.CompilerParams(vmem_limit_bytes=32 * 2**20),
    )(table, mine, other)


def assemble_attn_kernel(table_ref, mine_ref, other_ref, query_ref, out_ref, pair_ref):
    for slot in range(8):
        held = mine_ref if slot < 4 else other_ref
        piece = table_ref[slot]
        cols = pl.ds(pl.multiple_of(piece * LANES, LANES), LANES)
        block = held[slot % 4].astype(jnp.float32)
        query_ref[:, cols] = block[:, :LANES]
        out_ref[:, cols] = block[:, LANES : 2 * LANES]

        @pl.when(piece < 4)
        def _():
            pair_ref[:, cols] = block[:, 2 * LANES :]


def assemble_attn(mine, other):
    rows = mine.shape[1]
    return pl.pallas_call(
        assemble_attn_kernel,
        out_shape=[
            jax.ShapeDtypeStruct((rows, width * LANES), jnp.float32) for width in (8, 8, 4)
        ],
        in_specs=[pl.BlockSpec(memory_space=pltpu.SMEM)]
        + [pl.BlockSpec(memory_space=pltpu.VMEM)] * 2,
        out_specs=[pl.BlockSpec(memory_space=pltpu.VMEM)] * 3,
        compiler_params=pltpu.CompilerParams(vmem_limit_bytes=32 * 2**20),
    )(piece_table(), mine, other)


def to_slots(grad):
    return jnp.transpose(grad.reshape(grad.shape[0], -1, LANES), (1, 0, 2))


def unit_slots(*grads):
    return jnp.concatenate([to_slots(g) for g in grads], axis=2)


def unit_part(slots):
    return summed(exchanged(plus(slots[:4], swapped(slots[4:], "core")), "z"))


def unit_grads(parts, units):
    total = jnp.concatenate(parts, axis=1).reshape(8, 144, 3 * LANES)
    stack = exchanged(total, GROUP)
    stack = plus(stack, swapped(stack, "yl"))
    mine = gathered(stack, "z", 4)
    return assemble_units(mine, swapped(mine, "core"), units)


def attn_part(*grads):
    slots = jnp.concatenate([to_slots(g) for g in grads], axis=2)
    halves = slots.reshape((2, 4) + slots.shape[1:])
    core = lax.axis_index("core")
    total = plus(pick(halves, core), swapped(pick(halves, 1 - core), "core"))
    return summed(exchanged(total, "z"))


def attn_grads_of(query_pair, out):
    total = jnp.concatenate([query_pair[:, :LANES], out, query_pair[:, LANES:]], axis=1)
    total = summed(exchanged(total.reshape(8, 144, 3 * LANES), GROUP))
    total = plus(total, swapped(total, "yl"))
    mine = gathered(total, "z", 4)
    return assemble_attn(mine, swapped(mine, "core"))


def total_vector(vector):
    for axis in ("core", "yl", "yh"):
        vector = vector + swapped(vector, axis)
    for axis in ("z", "x"):
        for flip in (1, 2):
            vector = vector + lax.ppermute(vector, axis, [(i, i ^ flip) for i in range(4)])
    return vector


def norm_rows(entries, gain_row):
    return (
        entries
        * lax.rsqrt(jnp.mean(entries * entries, axis=-1, keepdims=True) + EPSILON)
        * gain_row
    )


def turn_tables(position_rows, head_width):
    half_width = head_width // 2
    frequency = ROPE_BASE ** (-2.0 * jnp.arange(half_width, dtype=jnp.float32) / head_width)
    angles = position_rows.astype(jnp.float32)[..., None] * frequency
    return (jnp.cos(angles), jnp.sin(angles))


def rotate(entries, cosine_table, sine_table):
    half_width = entries.shape[-1] // 2
    leading = entries[..., :half_width]
    trailing = entries[..., half_width:]
    return jnp.concatenate(
        [
            leading * cosine_table - trailing * sine_table,
            trailing * cosine_table + leading * sine_table,
        ],
        axis=-1,
    )


def query_piece(raw_proj, gain_row, cosine_table, sine_table):
    head_width = gain_row.shape[0]
    shaped = raw_proj.reshape(cosine_table.shape[0], cosine_table.shape[1], -1, head_width)
    turned = rotate(
        norm_rows(shaped, gain_row), cosine_table[:, :, None, :], sine_table[:, :, None, :]
    )
    return jnp.transpose(turned, (0, 2, 1, 3)) * head_width ** (-0.5)


def key_piece(raw_proj, gain_row, cosine_table, sine_table):
    shaped = raw_proj.reshape(cosine_table.shape[0], cosine_table.shape[1], gain_row.shape[0])
    return rotate(norm_rows(shaped, gain_row), cosine_table, sine_table)


def gelu_product(gate_proj, up_proj):
    return jax.nn.gelu(gate_proj, approximate=True) * up_proj


def masked_scores(queries, key_rows, allowed):
    plain = jnp.einsum("shqd,skd->shqk", queries, key_rows, preferred_element_type=jnp.float32)
    return jnp.where(allowed, plain, MASKED)


def transposed_product(left_side, right_side):
    return lax.dot_general(left_side, right_side, CONTRACT_ROWS, preferred_element_type=jnp.float32)


def product_by_rows(left_side, right_side):
    return lax.dot_general(left_side, right_side, CONTRACT_COLS, preferred_element_type=jnp.float32)


def local(
    tokens,
    positions,
    cotangent,
    gain_attn,
    gain_query,
    gain_key,
    gain_post_attn,
    gain_ffn,
    gain_post_ffn,
    w_query,
    w_key,
    w_value,
    w_out,
    w_gate,
    w_up,
    w_down,
):
    seq_count, tok_rows, model_width = tokens.shape
    all_rows = seq_count * tok_rows
    head_width = gain_query.shape[0]
    query_cols = w_query.shape[1]
    reach_back = min(-(-(WINDOW - 1) // tok_rows), 7)
    cosine_table, sine_table = turn_tables(positions, head_width)
    inputs = tokens.astype(jnp.float32).reshape(all_rows, model_width)
    normed_full, norm_attn_back = jax.vjp(norm_rows, inputs, gain_attn)
    normed = normed_full.astype(jnp.bfloat16)
    qkv_held = by_core(
        w_query[:, :768], jnp.concatenate([w_query[:, 768:], w_key, w_value], axis=1)
    )
    unit_held = unit_pieces(w_gate, w_up, w_down)
    qkv_mine = gathered(qkv_held, GROUP, 8).reshape(model_width, -1)
    qkv_other = swapped(qkv_mine, "core")
    out_held = by_core(w_out[:, :512], w_out[:, 512:])
    out_held, unit_held, _ = lax.optimization_barrier((out_held, unit_held, qkv_other))
    out_mine = gathered(out_held, GROUP, 8).reshape(model_width, -1)
    out_other = swapped(out_mine, "core")
    gate_cols, up_cols, down_cols = unit_shards(unit_held)
    first_raw, second_raw = both_cores(
        jnp.dot(normed, qkv_mine, preferred_element_type=jnp.float32),
        jnp.dot(normed, qkv_other, preferred_element_type=jnp.float32),
    )
    query_raw = jnp.concatenate([first_raw, second_raw[:, :256]], axis=1)
    key_raw = second_raw[:, 256:512]
    value_raw = second_raw[:, 512:]

    def query_local(raw_proj, gain_row):
        return query_piece(raw_proj, gain_row, cosine_table, sine_table)

    def key_local(raw_proj, gain_row):
        return key_piece(raw_proj, gain_row, cosine_table, sine_table)

    queries_full, query_back = jax.vjp(query_local, query_raw, gain_query)
    keys_full, key_back = jax.vjp(key_local, key_raw, gain_key)
    queries = queries_full.astype(jnp.bfloat16)
    local_pairs = jnp.concatenate(
        [keys_full, value_raw.reshape(seq_count, tok_rows, head_width)], axis=-1
    ).astype(jnp.bfloat16)
    collected = [local_pairs]
    for distance in range(1, reach_back + 1):
        collected.insert(0, from_behind(local_pairs, distance))
    pair_rows = jnp.concatenate(collected, axis=1)
    key_rows = pair_rows[..., :head_width]
    value_rows = pair_rows[..., head_width:]
    place_index = group_index()
    query_index = place_index * tok_rows + jnp.arange(tok_rows, dtype=jnp.int32)
    key_index = (place_index - reach_back) * tok_rows + jnp.arange(
        (reach_back + 1) * tok_rows, dtype=jnp.int32
    )
    offsets = query_index[:, None] - key_index[None, :]
    doc_start = query_index[None, :] - positions
    allowed = ((offsets >= 0) & (offsets < WINDOW))[None, :, :] & (
        key_index[None, None, :] >= doc_start[:, :, None]
    )
    allowed = allowed[:, None, :, :]
    scores = masked_scores(queries, key_rows, allowed)
    highest = jnp.max(scores, axis=-1, keepdims=True)
    exp_scores = jnp.exp(scores - highest)
    sum_scores = jnp.sum(exp_scores, axis=-1, keepdims=True)
    log_total = highest + jnp.log(sum_scores)
    weights = (exp_scores / sum_scores).astype(jnp.bfloat16)
    mixed_heads = jnp.einsum(
        "shqk,skd->sqhd", weights, value_rows, preferred_element_type=jnp.float32
    )
    attended = mixed_heads.reshape(all_rows, query_cols).astype(jnp.bfloat16)
    attended_mine, attended_other = both_cores(attended[:, :512], attended[:, 512:])
    attn_branch = product_by_rows(attended_mine, out_mine) + product_by_rows(
        attended_other, out_other
    )
    attn_normed, norm_post_attn_back = jax.vjp(norm_rows, attn_branch, gain_post_attn)
    middle = inputs + attn_normed
    ffn_in_full, norm_ffn_back = jax.vjp(norm_rows, middle, gain_ffn)
    normed_ffn = ffn_in_full.astype(jnp.bfloat16)
    ffn_rows = gather_tokens(normed_ffn)
    gate_proj = jnp.dot(ffn_rows, gate_cols, preferred_element_type=jnp.float32)
    up_proj = jnp.dot(ffn_rows, up_cols, preferred_element_type=jnp.float32)
    hidden_full, gelu_back = jax.vjp(gelu_product, gate_proj, up_proj)
    hidden = hidden_full.astype(jnp.bfloat16)
    ffn_branch = scatter_tokens(product_by_rows(hidden, down_cols))
    ffn_normed, norm_post_ffn_back = jax.vjp(norm_rows, ffn_branch, gain_post_ffn)
    outputs = (middle + ffn_normed).astype(jnp.bfloat16).reshape(seq_count, tok_rows, model_width)
    upstream = cotangent.astype(jnp.float32).reshape(all_rows, model_width)
    grad_ffn_branch, grad_post_ffn = norm_post_ffn_back(upstream)
    grad_ffn_branch = grad_ffn_branch.astype(jnp.bfloat16)
    grad_branch_rows = gather_tokens(grad_ffn_branch)
    grad_hidden = jnp.dot(grad_branch_rows, down_cols, preferred_element_type=jnp.float32)
    grad_gate_full, grad_up_full = gelu_back(grad_hidden)
    grad_gate_part = grad_gate_full.astype(jnp.bfloat16)
    grad_up_part = grad_up_full.astype(jnp.bfloat16)
    grad_partial = product_by_rows(grad_gate_part, gate_cols) + product_by_rows(
        grad_up_part, up_cols
    )
    grad_normed_ffn = scatter_tokens(grad_partial)
    ffn_rows, grad_branch_rows, _ = lax.optimization_barrier(
        (ffn_rows, grad_branch_rows, grad_partial)
    )
    down_part = unit_part(
        unit_slots(transposed_product(grad_branch_rows, hidden).astype(jnp.bfloat16))
    )
    gate_up_part = unit_part(
        unit_slots(
            transposed_product(ffn_rows, grad_gate_part).astype(jnp.bfloat16),
            transposed_product(ffn_rows, grad_up_part).astype(jnp.bfloat16),
        )
    )
    grad_gate_total, grad_up_total, grad_down_total = unit_grads(
        (gate_up_part, down_part), w_gate.shape[1]
    )
    grad_middle_part, grad_gain_ffn = norm_ffn_back(grad_normed_ffn)
    grad_middle = upstream + grad_middle_part
    grad_attn_branch, grad_post_attn = norm_post_attn_back(grad_middle)
    grad_attn_branch = grad_attn_branch.astype(jnp.bfloat16)
    out_part = attn_part(
        transposed_product(grad_attn_branch, attended).astype(jnp.bfloat16)
    )
    grad_attended = jnp.concatenate(
        both_cores(
            jnp.dot(grad_attn_branch, out_mine, preferred_element_type=jnp.float32),
            jnp.dot(grad_attn_branch, out_other, preferred_element_type=jnp.float32),
        ),
        axis=1,
    )
    grad_heads = grad_attended.astype(jnp.bfloat16).reshape(seq_count, tok_rows, HEADS, head_width)
    scores = masked_scores(queries, key_rows, allowed)
    probabilities = jnp.exp(scores - log_total)
    grad_probs = jnp.einsum(
        "sqhd,skd->shqk", grad_heads, value_rows, preferred_element_type=jnp.float32
    )
    centre = jnp.sum(probabilities * grad_probs, axis=-1, keepdims=True)
    grad_scores = (probabilities * (grad_probs - centre)).astype(jnp.bfloat16)
    grad_queries = jnp.einsum(
        "shqk,skd->shqd", grad_scores, key_rows, preferred_element_type=jnp.float32
    )
    grad_key_rows = jnp.einsum(
        "shqk,shqd->skd", grad_scores, queries, preferred_element_type=jnp.float32
    )
    grad_value_rows = jnp.einsum(
        "shqk,sqhd->skd",
        probabilities.astype(jnp.bfloat16),
        grad_heads,
        preferred_element_type=jnp.float32,
    )
    grad_pairs = jnp.concatenate([grad_key_rows, grad_value_rows], axis=-1)
    own_pairs = grad_pairs[:, reach_back * tok_rows :]
    for distance in range(1, reach_back + 1):
        lower_block = reach_back - distance
        sent_block = grad_pairs[:, lower_block * tok_rows : (lower_block + 1) * tok_rows]
        own_pairs = own_pairs + from_behind(
            sent_block.astype(jnp.bfloat16), -distance
        ).astype(sent_block.dtype)
    grad_key_raw, grad_gain_key = key_back(own_pairs[..., :head_width])
    grad_query_raw, grad_gain_query = query_back(grad_queries)
    grad_value_raw = own_pairs[..., head_width:].reshape(all_rows, head_width)
    grad_projected = jnp.concatenate([grad_query_raw, grad_key_raw, grad_value_raw], axis=1).astype(
        jnp.bfloat16
    )
    projected_mine, projected_other = both_cores(grad_projected[:, :768], grad_projected[:, 768:])
    contribution = product_by_rows(projected_mine, qkv_mine) + product_by_rows(
        projected_other, qkv_other
    )
    projected_part = transposed_product(normed, grad_projected).astype(jnp.bfloat16)
    query_total, grad_out_total, pair_total = attn_grads_of(
        attn_part(
            projected_part[:, :query_cols],
            jnp.pad(projected_part[:, query_cols:], ((0, 0), (0, 512))),
        ),
        out_part,
    )
    grad_inputs_part, grad_gain_attn = norm_attn_back(contribution)
    grad_tokens = (grad_middle + grad_inputs_part).reshape(seq_count, tok_rows, model_width)
    gains = total_vector(
        jnp.concatenate(
            [
                grad_gain_attn,
                grad_gain_query,
                grad_gain_key,
                grad_post_attn,
                grad_gain_ffn,
                grad_post_ffn,
            ]
        )
    )
    query_at, key_at = model_width, model_width + head_width
    wide_at = key_at + head_width
    return (
        outputs,
        grad_tokens,
        gains[:query_at],
        gains[query_at:key_at],
        gains[key_at:wide_at],
        gains[wide_at : wide_at + model_width],
        gains[wide_at + model_width : wide_at + 2 * model_width],
        gains[wide_at + 2 * model_width :],
        query_total,
        pair_total[:, :head_width],
        pair_total[:, head_width:],
        grad_out_total,
        grad_gate_total,
        grad_up_total,
        grad_down_total,
    )


def solution(mesh):
    fine = Mesh(mesh.devices.reshape(4, 2, 4, 2, 2), GROUP + REPLICA)
    placed = (
        P(REPLICA, GROUP, None),
        P(REPLICA, GROUP),
        P(REPLICA, GROUP, None),
        P(),
        P(),
        P(),
        P(),
        P(),
        P(),
        P(GROUP, None),
        P(GROUP, None),
        P(GROUP, None),
        P(GROUP, None),
        P(GROUP, None),
        P(GROUP, None),
        P(GROUP, None),
    )
    return jax.shard_map(
        local,
        mesh=fine,
        in_specs=placed,
        out_specs=(
            P(REPLICA, GROUP, None),
            P(REPLICA, GROUP, None),
            P(),
            P(),
            P(),
            P(),
            P(),
            P(),
            P(GROUP, None),
            P(GROUP, None),
            P(GROUP, None),
            P(GROUP, None),
            P(GROUP, None),
            P(GROUP, None),
            P(GROUP, None),
        ),
        check_vma=False,
    )
```

```python
import jax
import jax.numpy as jnp
from jax import lax
from jax.experimental import pallas as pl
from jax.experimental.pallas import tpu as pltpu
from jax.sharding import Mesh
from jax.sharding import PartitionSpec as P

HEADS = 4
WINDOW = 512


EPSILON = 1e-06
ROPE_BASE = 10000.0
MASKED = -1e30
CONTRACT_COLS = (((1,), (1,)), ((), ()))
CONTRACT_ROWS = (((0,), (0,)), ((), ()))


GROUP = ("x", "yh")
REPLICA = ("z", "yl", "core")
SHIFTS = ((1, 0), (3, 0), (0, 1), (1, 1), (3, 1), (2, 0), (2, 1))
Z_STEPS = (1, 3, 2)
LANES = 128
UNIT_TILES = 7


def from_behind(block, distance):
    devices = range(8)
    route = [(i - distance, i) for i in devices if i - distance in devices]
    return lax.ppermute(block, GROUP, route)


def shifted(block, step):
    route = [(a * 2 + b, (a + step[0]) % 4 * 2 + (b ^ step[1])) for a in range(4) for b in range(2)]
    return lax.ppermute(block, GROUP, route)


def turned(block, axis, step, size):
    return lax.ppermute(block, axis, [(i, (i + step) % size) for i in range(size)])


def swapped(block, axis):
    return turned(block, axis, 1, 2)


def pick(stack, index):
    return lax.dynamic_index_in_dim(stack, index, 0, keepdims=False)


def place(stack, block, index):
    return lax.dynamic_update_index_in_dim(stack, block, index, 0)


def along_z():
    depth = lax.axis_index("z")
    return [lax.rem(depth + 4 - step, 4) for step in (0,) + Z_STEPS]


def gathered_z(block):
    return [block] + [turned(block, "z", step, 4) for step in Z_STEPS]


def after(value, other):
    return lax.optimization_barrier((value, other))[0]


def group_index():
    return lax.axis_index("x") * 2 + lax.axis_index("yh")


def exchanged(stack, axes):
    return lax.all_to_all(stack, axes, 0, 0)


def gathered(block, axes, size):
    return exchanged(jnp.broadcast_to(block, (size,) + block.shape), axes)


def on_first_core():
    return lax.axis_index("core") == 0


def by_core(first, second):
    return jnp.where(on_first_core(), first, second)


def both_cores(mine, other):
    return by_core(mine, other), by_core(other, mine)


def gather_tokens(rows):
    blocks = [rows] + [shifted(rows, step) for step in SHIFTS]
    return jnp.concatenate(blocks, axis=0), blocks[1]


def scatter_tokens(partial):
    rows = partial.shape[0] // 8
    total = partial[:rows]
    blocks = []
    for i, step in enumerate(SHIFTS):
        back = ((4 - step[0]) % 4, step[1])
        block = partial[(i + 1) * rows : (i + 2) * rows].astype(jnp.bfloat16)
        blocks.append(shifted(block, back))
    for block in blocks:
        total = total + block.astype(jnp.float32)
    return total


def piece_table():
    core = lax.axis_index("core")
    return jnp.stack([half * 4 + z for half in (core, 1 - core) for z in along_z()])


def unit_kernel(piece_ref, gate_ref, up_ref, down_ref, out_ref):
    piece = piece_ref[0]
    real = (piece < UNIT_TILES) & (pl.program_id(0) * UNIT_TILES + piece < piece_ref[1])
    for i, ref in enumerate((gate_ref, up_ref, down_ref)):
        block = ref[...]
        out_ref[0, :, i * LANES : (i + 1) * LANES] = jnp.where(real, block, jnp.zeros_like(block))


def unit_pieces(w_gate, w_up, w_down):
    rows, units = w_gate.shape
    tiles = units // LANES
    piece = lax.axis_index("core") * 4 + lax.axis_index("z")
    numbers = jnp.stack([piece, jnp.int32(tiles)])
    spec = pl.BlockSpec(
        (rows, LANES), lambda j, num: (0, jnp.minimum(j * UNIT_TILES + num[0], tiles - 1))
    )
    return pl.pallas_call(
        unit_kernel,
        out_shape=jax.ShapeDtypeStruct((8, rows, 3 * LANES), jnp.bfloat16),
        grid_spec=pltpu.PrefetchScalarGridSpec(
            num_scalar_prefetch=1,
            grid=(8,),
            in_specs=[spec] * 3,
            out_specs=pl.BlockSpec((1, rows, 3 * LANES), lambda j, num: (j, 0, 0)),
        ),
    )(numbers, w_gate, w_up, w_down)


def unit_shards(blocks):
    mine = jnp.zeros((4,) + blocks[0].shape, blocks[0].dtype)
    for block, z in zip(blocks, along_z()):
        mine = place(mine, block, z)
    other = swapped(mine, "core")
    slots = [mine[i] for i in range(4)] + [other[i] for i in range(4)]
    return tuple(
        jnp.concatenate([slot[:, i * LANES : (i + 1) * LANES] for slot in slots], axis=1)
        for i in range(3)
    )


def plus(*blocks):
    return sum(block.astype(jnp.float32) for block in blocks).astype(jnp.bfloat16)


def summed(stack):
    return jnp.sum(stack.astype(jnp.float32), axis=0).astype(jnp.bfloat16)


def assemble_units_kernel(table_ref, mine_ref, other_ref, *out_refs):
    for slot in range(8):
        held = mine_ref if slot < 4 else other_ref
        piece = table_ref[slot]

        @pl.when(piece < UNIT_TILES)
        def _():
            cols = pl.ds(pl.multiple_of(piece * LANES, LANES), LANES)
            for i, out_ref in enumerate(out_refs):
                block = held[slot % 4, 0, :, i * LANES : (i + 1) * LANES]
                out_ref[:, cols] = block.astype(jnp.float32)


def assemble_units(mine, other, units):
    rows = mine.shape[2]
    table = piece_table()
    block = UNIT_TILES * LANES
    spec = pl.BlockSpec((4, 1, rows, 3 * LANES), lambda r, table: (0, r, 0, 0))
    return pl.pallas_call(
        assemble_units_kernel,
        out_shape=[jax.ShapeDtypeStruct((rows, units), jnp.float32)] * 3,
        grid_spec=pltpu.PrefetchScalarGridSpec(
            num_scalar_prefetch=1,
            grid=(8,),
            in_specs=[spec] * 2,
            out_specs=[pl.BlockSpec((rows, block), lambda r, table: (0, r))] * 3,
        ),
        compiler_params=pltpu.CompilerParams(vmem_limit_bytes=32 * 2**20),
    )(table, mine, other)


def assemble_attn_kernel(table_ref, mine_ref, other_ref, query_ref, out_ref, pair_ref):
    for slot in range(8):
        held = mine_ref if slot < 4 else other_ref
        piece = table_ref[slot]
        cols = pl.ds(pl.multiple_of(piece * LANES, LANES), LANES)
        block = held[slot % 4].astype(jnp.float32)
        query_ref[:, cols] = block[:, :LANES]
        out_ref[:, cols] = block[:, LANES : 2 * LANES]

        @pl.when(piece < 4)
        def _():
            pair_ref[:, cols] = block[:, 2 * LANES :]


def assemble_attn(mine, other):
    rows = mine.shape[1]
    return pl.pallas_call(
        assemble_attn_kernel,
        out_shape=[
            jax.ShapeDtypeStruct((rows, width * LANES), jnp.float32) for width in (8, 8, 4)
        ],
        in_specs=[pl.BlockSpec(memory_space=pltpu.SMEM)]
        + [pl.BlockSpec(memory_space=pltpu.VMEM)] * 2,
        out_specs=[pl.BlockSpec(memory_space=pltpu.VMEM)] * 3,
        compiler_params=pltpu.CompilerParams(vmem_limit_bytes=32 * 2**20),
    )(piece_table(), mine, other)


def to_slots(grad):
    return jnp.transpose(grad.reshape(grad.shape[0], -1, LANES), (1, 0, 2))


def unit_slots(*grads):
    return jnp.concatenate([to_slots(g) for g in grads], axis=2)


def unit_halves(slots):
    return plus(slots[:4], swapped(slots[4:], "core"))


def unit_blocks(part):
    return exchanged(part.reshape(8, 144, 3 * LANES), GROUP)


def unit_grads(blocks, units):
    mine = jnp.stack(blocks)
    return assemble_units(mine, swapped(mine, "core"), units)


def attn_halves(*grads):
    slots = jnp.concatenate([to_slots(g) for g in grads], axis=2)
    halves = slots.reshape((2, 4) + slots.shape[1:])
    core = lax.axis_index("core")
    return plus(pick(halves, core), swapped(pick(halves, 1 - core), "core"))


def attn_total(blocks):
    total = summed(blocks)
    return plus(total, swapped(total, "yl"))


def attn_grads_of(total):
    mine = jnp.stack(gathered_z(total))
    return assemble_attn(mine, swapped(mine, "core"))


def along(vector, axis):
    if lax.axis_size(axis) == 2:
        return vector + swapped(vector, axis)
    for flip in (1, 2):
        vector = vector + lax.ppermute(vector, axis, [(i, i ^ flip) for i in range(4)])
    return vector


def norm_rows(entries, gain_row):
    return (
        entries
        * lax.rsqrt(jnp.mean(entries * entries, axis=-1, keepdims=True) + EPSILON)
        * gain_row
    )


def turn_tables(position_rows, head_width):
    half_width = head_width // 2
    frequency = ROPE_BASE ** (-2.0 * jnp.arange(half_width, dtype=jnp.float32) / head_width)
    angles = position_rows.astype(jnp.float32)[..., None] * frequency
    return (jnp.cos(angles), jnp.sin(angles))


def rotate(entries, cosine_table, sine_table):
    half_width = entries.shape[-1] // 2
    leading = entries[..., :half_width]
    trailing = entries[..., half_width:]
    return jnp.concatenate(
        [
            leading * cosine_table - trailing * sine_table,
            trailing * cosine_table + leading * sine_table,
        ],
        axis=-1,
    )


def query_piece(raw_proj, gain_row, cosine_table, sine_table):
    head_width = gain_row.shape[0]
    shaped = raw_proj.reshape(cosine_table.shape[0], cosine_table.shape[1], -1, head_width)
    turned = rotate(
        norm_rows(shaped, gain_row), cosine_table[:, :, None, :], sine_table[:, :, None, :]
    )
    return jnp.transpose(turned, (0, 2, 1, 3)) * head_width ** (-0.5)


def key_piece(raw_proj, gain_row, cosine_table, sine_table):
    shaped = raw_proj.reshape(cosine_table.shape[0], cosine_table.shape[1], gain_row.shape[0])
    return rotate(norm_rows(shaped, gain_row), cosine_table, sine_table)


def gelu_product(gate_proj, up_proj):
    return jax.nn.gelu(gate_proj, approximate=True) * up_proj


def masked_scores(queries, key_rows, allowed):
    plain = jnp.einsum("shqd,skd->shqk", queries, key_rows, preferred_element_type=jnp.float32)
    return jnp.where(allowed, plain, MASKED)


def transposed_product(left_side, right_side):
    return lax.dot_general(left_side, right_side, CONTRACT_ROWS, preferred_element_type=jnp.float32)


def product_by_rows(left_side, right_side):
    return lax.dot_general(left_side, right_side, CONTRACT_COLS, preferred_element_type=jnp.float32)


def local(
    tokens,
    positions,
    cotangent,
    gain_attn,
    gain_query,
    gain_key,
    gain_post_attn,
    gain_ffn,
    gain_post_ffn,
    w_query,
    w_key,
    w_value,
    w_out,
    w_gate,
    w_up,
    w_down,
):
    seq_count, tok_rows, model_width = tokens.shape
    all_rows = seq_count * tok_rows
    head_width = gain_query.shape[0]
    query_cols = w_query.shape[1]
    reach_back = min(-(-(WINDOW - 1) // tok_rows), 7)
    cosine_table, sine_table = turn_tables(positions, head_width)
    inputs = tokens.astype(jnp.float32).reshape(all_rows, model_width)
    normed_full, norm_attn_back = jax.vjp(norm_rows, inputs, gain_attn)
    normed = normed_full.astype(jnp.bfloat16)
    qkv_held = by_core(
        w_query[:, :768], jnp.concatenate([w_query[:, 768:], w_key, w_value], axis=1)
    )
    unit_held = unit_pieces(w_gate, w_up, w_down)
    qkv_mine = gathered(qkv_held, GROUP, 8).reshape(model_width, -1)
    qkv_other = swapped(qkv_mine, "core")
    out_held = by_core(w_out[:, :512], w_out[:, 512:])
    unit_stack = exchanged(after(unit_held, qkv_mine), GROUP).reshape(model_width, -1)
    first_raw, second_raw = both_cores(
        jnp.dot(normed, qkv_mine, preferred_element_type=jnp.float32),
        jnp.dot(normed, qkv_other, preferred_element_type=jnp.float32),
    )
    query_raw = jnp.concatenate([first_raw, second_raw[:, :256]], axis=1)
    key_raw = second_raw[:, 256:512]
    value_raw = second_raw[:, 512:]

    def query_local(raw_proj, gain_row):
        return query_piece(raw_proj, gain_row, cosine_table, sine_table)

    def key_local(raw_proj, gain_row):
        return key_piece(raw_proj, gain_row, cosine_table, sine_table)

    queries_full, query_back = jax.vjp(query_local, query_raw, gain_query)
    keys_full, key_back = jax.vjp(key_local, key_raw, gain_key)
    queries = queries_full.astype(jnp.bfloat16)
    local_pairs = jnp.concatenate(
        [keys_full, value_raw.reshape(seq_count, tok_rows, head_width)], axis=-1
    ).astype(jnp.bfloat16)
    out_mine = gathered(after(out_held, (unit_stack, local_pairs)), GROUP, 8)
    out_mine = out_mine.reshape(model_width, -1)
    out_other = swapped(out_mine, "core")
    collected = [local_pairs]
    for distance in range(1, reach_back + 1):
        collected.insert(0, from_behind(local_pairs, distance))
    pair_rows = jnp.concatenate(collected, axis=1)
    key_rows = pair_rows[..., :head_width]
    value_rows = pair_rows[..., head_width:]
    place_index = group_index()
    query_index = place_index * tok_rows + jnp.arange(tok_rows, dtype=jnp.int32)
    key_index = (place_index - reach_back) * tok_rows + jnp.arange(
        (reach_back + 1) * tok_rows, dtype=jnp.int32
    )
    offsets = query_index[:, None] - key_index[None, :]
    doc_start = query_index[None, :] - positions
    allowed = ((offsets >= 0) & (offsets < WINDOW))[None, :, :] & (
        key_index[None, None, :] >= doc_start[:, :, None]
    )
    allowed = allowed[:, None, :, :]
    scores = masked_scores(queries, key_rows, allowed)
    highest = jnp.max(scores, axis=-1, keepdims=True)
    exp_scores = jnp.exp(scores - highest)
    sum_scores = jnp.sum(exp_scores, axis=-1, keepdims=True)
    log_total = highest + jnp.log(sum_scores)
    weights = (exp_scores / sum_scores).astype(jnp.bfloat16)
    mixed_heads = jnp.einsum(
        "shqk,skd->sqhd", weights, value_rows, preferred_element_type=jnp.float32
    )
    attended = mixed_heads.reshape(all_rows, query_cols).astype(jnp.bfloat16)
    unit_blocks_z = gathered_z(after(unit_stack, pair_rows))
    attended_mine, attended_other = both_cores(attended[:, :512], attended[:, 512:])
    attn_branch = product_by_rows(attended_mine, out_mine) + product_by_rows(
        attended_other, out_other
    )
    attn_normed, norm_post_attn_back = jax.vjp(norm_rows, attn_branch, gain_post_attn)
    middle = inputs + attn_normed
    ffn_in_full, norm_ffn_back = jax.vjp(norm_rows, middle, gain_ffn)
    normed_ffn = ffn_in_full.astype(jnp.bfloat16)
    ffn_rows, ffn_block = gather_tokens(normed_ffn)
    gate_cols, up_cols, down_cols = unit_shards(after(unit_blocks_z, ffn_block))
    gate_proj = jnp.dot(ffn_rows, gate_cols, preferred_element_type=jnp.float32)
    up_proj = jnp.dot(ffn_rows, up_cols, preferred_element_type=jnp.float32)
    hidden_full, gelu_back = jax.vjp(gelu_product, gate_proj, up_proj)
    hidden = hidden_full.astype(jnp.bfloat16)
    ffn_branch = scatter_tokens(product_by_rows(hidden, down_cols))
    ffn_normed, norm_post_ffn_back = jax.vjp(norm_rows, ffn_branch, gain_post_ffn)
    outputs = (middle + ffn_normed).astype(jnp.bfloat16).reshape(seq_count, tok_rows, model_width)
    upstream = cotangent.astype(jnp.float32).reshape(all_rows, model_width)
    grad_ffn_branch, grad_post_ffn = norm_post_ffn_back(upstream)
    grad_ffn_branch = grad_ffn_branch.astype(jnp.bfloat16)
    grad_branch_rows, _ = gather_tokens(grad_ffn_branch)
    grad_hidden = jnp.dot(grad_branch_rows, down_cols, preferred_element_type=jnp.float32)
    grad_gate_full, grad_up_full = gelu_back(grad_hidden)
    grad_gate_part = grad_gate_full.astype(jnp.bfloat16)
    grad_up_part = grad_up_full.astype(jnp.bfloat16)
    grad_partial = product_by_rows(grad_gate_part, gate_cols) + product_by_rows(
        grad_up_part, up_cols
    )
    grad_normed_ffn = scatter_tokens(grad_partial)
    ffn_rows, grad_branch_rows, _ = lax.optimization_barrier(
        (ffn_rows, grad_branch_rows, grad_normed_ffn)
    )
    own_halves = unit_halves(
        unit_slots(
            transposed_product(ffn_rows, grad_gate_part).astype(jnp.bfloat16),
            transposed_product(ffn_rows, grad_up_part).astype(jnp.bfloat16),
            transposed_product(grad_branch_rows, hidden).astype(jnp.bfloat16),
        )
    )
    own_part = summed(exchanged(own_halves, "z"))
    grad_middle_part, grad_gain_ffn = norm_ffn_back(grad_normed_ffn)
    grad_middle = upstream + grad_middle_part
    grad_attn_branch, grad_post_attn = norm_post_attn_back(grad_middle)
    grad_attn_branch = after(grad_attn_branch.astype(jnp.bfloat16), own_halves)
    out_halves = attn_halves(
        transposed_product(grad_attn_branch, attended).astype(jnp.bfloat16)
    )
    grad_attended = jnp.concatenate(
        both_cores(
            jnp.dot(grad_attn_branch, out_mine, preferred_element_type=jnp.float32),
            jnp.dot(grad_attn_branch, out_other, preferred_element_type=jnp.float32),
        ),
        axis=1,
    )
    grad_heads = grad_attended.astype(jnp.bfloat16).reshape(seq_count, tok_rows, HEADS, head_width)
    scores = masked_scores(queries, key_rows, allowed)
    probabilities = jnp.exp(scores - log_total)
    grad_probs = jnp.einsum(
        "sqhd,skd->shqk", grad_heads, value_rows, preferred_element_type=jnp.float32
    )
    centre = jnp.sum(probabilities * grad_probs, axis=-1, keepdims=True)
    grad_scores = (probabilities * (grad_probs - centre)).astype(jnp.bfloat16)
    grad_queries = jnp.einsum(
        "shqk,skd->shqd", grad_scores, key_rows, preferred_element_type=jnp.float32
    )
    grad_key_rows = jnp.einsum(
        "shqk,shqd->skd", grad_scores, queries, preferred_element_type=jnp.float32
    )
    grad_value_rows = jnp.einsum(
        "shqk,sqhd->skd",
        probabilities.astype(jnp.bfloat16),
        grad_heads,
        preferred_element_type=jnp.float32,
    )
    grad_pairs = jnp.concatenate([grad_key_rows, grad_value_rows], axis=-1)
    own_blocks = unit_blocks(after(own_part, grad_pairs))
    own_pairs = grad_pairs[:, reach_back * tok_rows :]
    for distance in range(1, reach_back + 1):
        lower_block = reach_back - distance
        sent_block = grad_pairs[:, lower_block * tok_rows : (lower_block + 1) * tok_rows]
        own_pairs = own_pairs + from_behind(
            sent_block.astype(jnp.bfloat16), -distance
        ).astype(sent_block.dtype)
    grad_key_raw, grad_gain_key = key_back(own_pairs[..., :head_width])
    grad_query_raw, grad_gain_query = query_back(grad_queries)
    grad_value_raw = own_pairs[..., head_width:].reshape(all_rows, head_width)
    grad_projected = jnp.concatenate([grad_query_raw, grad_key_raw, grad_value_raw], axis=1).astype(
        jnp.bfloat16
    )
    late_projected = after(grad_projected, own_blocks)
    projected_mine, projected_other = both_cores(late_projected[:, :768], late_projected[:, 768:])
    contribution = product_by_rows(projected_mine, qkv_mine) + product_by_rows(
        projected_other, qkv_other
    )
    projected_part = transposed_product(normed, after(grad_projected, own_part)).astype(
        jnp.bfloat16
    )
    qkv_halves = attn_halves(
        projected_part[:, :query_cols],
        jnp.pad(projected_part[:, query_cols:], ((0, 0), (0, 512))),
    )
    grad_inputs_part, grad_gain_attn = norm_attn_back(contribution)
    grad_tokens = (grad_middle + grad_inputs_part).reshape(seq_count, tok_rows, model_width)
    gains = along(
        jnp.concatenate(
            [
                grad_gain_attn,
                grad_gain_query,
                grad_gain_key,
                grad_post_attn,
                grad_gain_ffn,
                grad_post_ffn,
            ]
        ),
        "z",
    )
    attn_pieces = jnp.concatenate(
        [qkv_halves[..., :LANES], out_halves, qkv_halves[..., LANES:]], axis=2
    )
    attn_pieces = exchanged(after(attn_pieces, (own_blocks, gains)), "z")
    for axis in ("core", "yl", "x", "yh"):
        gains = along(gains, axis)
    attn_pieces = after(attn_pieces, gains)
    attn_blocks = exchanged(summed(attn_pieces).reshape(8, 144, 3 * LANES), GROUP)
    own_blocks = plus(own_blocks, swapped(own_blocks, "yl"))
    attn_sum = attn_total(attn_blocks)
    own_gathered = gathered_z(after(own_blocks, attn_pieces))
    grad_gate_total, grad_up_total, grad_down_total = unit_grads(
        after(own_gathered, attn_sum), w_gate.shape[1]
    )
    query_total, grad_out_total, pair_total = attn_grads_of(attn_sum)
    query_at, key_at = model_width, model_width + head_width
    wide_at = key_at + head_width
    return (
        outputs,
        grad_tokens,
        gains[:query_at],
        gains[query_at:key_at],
        gains[key_at:wide_at],
        gains[wide_at : wide_at + model_width],
        gains[wide_at + model_width : wide_at + 2 * model_width],
        gains[wide_at + 2 * model_width :],
        query_total,
        pair_total[:, :head_width],
        pair_total[:, head_width:],
        grad_out_total,
        grad_gate_total,
        grad_up_total,
        grad_down_total,
    )


def solution(mesh):
    fine = Mesh(mesh.devices.reshape(4, 2, 4, 2, 2), GROUP + REPLICA)
    placed = (
        P(REPLICA, GROUP, None),
        P(REPLICA, GROUP),
        P(REPLICA, GROUP, None),
        P(),
        P(),
        P(),
        P(),
        P(),
        P(),
        P(GROUP, None),
        P(GROUP, None),
        P(GROUP, None),
        P(GROUP, None),
        P(GROUP, None),
        P(GROUP, None),
        P(GROUP, None),
    )
    return jax.shard_map(
        local,
        mesh=fine,
        in_specs=placed,
        out_specs=(
            P(REPLICA, GROUP, None),
            P(REPLICA, GROUP, None),
            P(),
            P(),
            P(),
            P(),
            P(),
            P(),
            P(GROUP, None),
            P(GROUP, None),
            P(GROUP, None),
            P(GROUP, None),
            P(GROUP, None),
            P(GROUP, None),
            P(GROUP, None),
        ),
        check_vma=False,
    )
```

```python
import jax
import jax.numpy as jnp
from jax import lax
from jax.experimental import pallas as pl
from jax.experimental.pallas import tpu as pltpu
from jax.sharding import Mesh
from jax.sharding import PartitionSpec as P

HEADS = 4
WINDOW = 512


EPSILON = 1e-06
ROPE_BASE = 10000.0
MASKED = -1e30
CONTRACT_COLS = (((1,), (1,)), ((), ()))
CONTRACT_ROWS = (((0,), (0,)), ((), ()))


GROUP = ("x", "yh")
REPLICA = ("z", "yl", "core")
SHIFTS = ((1, 0), (3, 0), (0, 1), (1, 1), (3, 1), (2, 0), (2, 1))
Z_STEPS = (1, 3, 2)
LANES = 128
UNIT_TILES = 7


def from_behind(block, distance):
    devices = range(8)
    route = [(i - distance, i) for i in devices if i - distance in devices]
    return lax.ppermute(block, GROUP, route)


def shifted(block, step):
    route = [(a * 2 + b, (a + step[0]) % 4 * 2 + (b ^ step[1])) for a in range(4) for b in range(2)]
    return lax.ppermute(block, GROUP, route)


def turned(block, axis, step, size):
    return lax.ppermute(block, axis, [(i, (i + step) % size) for i in range(size)])


def swapped(block, axis):
    return turned(block, axis, 1, 2)


def pick(stack, index):
    return lax.dynamic_index_in_dim(stack, index, 0, keepdims=False)


def place(stack, block, index):
    return lax.dynamic_update_index_in_dim(stack, block, index, 0)


def along_z():
    depth = lax.axis_index("z")
    return [lax.rem(depth + 4 - step, 4) for step in (0,) + Z_STEPS]


def gathered_z(block):
    return [block] + [turned(block, "z", step, 4) for step in Z_STEPS]


def after(value, other):
    return lax.optimization_barrier((value, other))[0]


def group_index():
    return lax.axis_index("x") * 2 + lax.axis_index("yh")


def exchanged(stack, axes):
    return lax.all_to_all(stack, axes, 0, 0)


def gathered(block, axes, size):
    return exchanged(jnp.broadcast_to(block, (size,) + block.shape), axes)


def on_first_core():
    return lax.axis_index("core") == 0


def by_core(first, second):
    return jnp.where(on_first_core(), first, second)


def both_cores(mine, other):
    return by_core(mine, other), by_core(other, mine)


def gather_tokens(rows):
    blocks = [rows] + [shifted(rows, step) for step in SHIFTS]
    return jnp.concatenate(blocks, axis=0), blocks[1]


def scatter_tokens(partial):
    rows = partial.shape[0] // 8
    total = partial[:rows]
    blocks = []
    for i, step in enumerate(SHIFTS):
        back = ((4 - step[0]) % 4, step[1])
        block = partial[(i + 1) * rows : (i + 2) * rows].astype(jnp.bfloat16)
        blocks.append(shifted(block, back))
    for block in blocks:
        total = total + block.astype(jnp.float32)
    return total


def piece_table():
    core = lax.axis_index("core")
    return jnp.stack([half * 4 + z for half in (core, 1 - core) for z in along_z()])


def unit_kernel(piece_ref, gate_ref, up_ref, down_ref, out_ref):
    piece = piece_ref[0]
    real = (piece < UNIT_TILES) & (pl.program_id(0) * UNIT_TILES + piece < piece_ref[1])
    for i, ref in enumerate((gate_ref, up_ref, down_ref)):
        block = ref[...]
        out_ref[0, :, i * LANES : (i + 1) * LANES] = jnp.where(real, block, jnp.zeros_like(block))


def unit_pieces(w_gate, w_up, w_down):
    rows, units = w_gate.shape
    tiles = units // LANES
    piece = lax.axis_index("core") * 4 + lax.axis_index("z")
    numbers = jnp.stack([piece, jnp.int32(tiles)])
    spec = pl.BlockSpec(
        (rows, LANES), lambda j, num: (0, jnp.minimum(j * UNIT_TILES + num[0], tiles - 1))
    )
    return pl.pallas_call(
        unit_kernel,
        out_shape=jax.ShapeDtypeStruct((8, rows, 3 * LANES), jnp.bfloat16),
        grid_spec=pltpu.PrefetchScalarGridSpec(
            num_scalar_prefetch=1,
            grid=(8,),
            in_specs=[spec] * 3,
            out_specs=pl.BlockSpec((1, rows, 3 * LANES), lambda j, num: (j, 0, 0)),
        ),
    )(numbers, w_gate, w_up, w_down)


def unit_shards(blocks):
    mine = jnp.zeros((4,) + blocks[0].shape, blocks[0].dtype)
    for block, z in zip(blocks, along_z()):
        mine = place(mine, block, z)
    other = swapped(mine, "core")
    slots = [mine[i] for i in range(4)] + [other[i] for i in range(4)]
    return tuple(
        jnp.concatenate([slot[:, i * LANES : (i + 1) * LANES] for slot in slots], axis=1)
        for i in range(3)
    )


def plus(*blocks):
    return sum(block.astype(jnp.float32) for block in blocks).astype(jnp.bfloat16)


def summed(stack):
    return jnp.sum(stack.astype(jnp.float32), axis=0).astype(jnp.bfloat16)


def assemble_units_kernel(table_ref, mine_ref, other_ref, *out_refs):
    for slot in range(8):
        held = mine_ref if slot < 4 else other_ref
        piece = table_ref[slot]

        @pl.when(piece < UNIT_TILES)
        def _():
            cols = pl.ds(pl.multiple_of(piece * LANES, LANES), LANES)
            for i, out_ref in enumerate(out_refs):
                block = held[slot % 4, 0, :, i * LANES : (i + 1) * LANES]
                out_ref[:, cols] = block.astype(jnp.float32)


def assemble_units(mine, other, units):
    rows = mine.shape[2]
    table = piece_table()
    block = UNIT_TILES * LANES
    spec = pl.BlockSpec((4, 1, rows, 3 * LANES), lambda r, table: (0, r, 0, 0))
    return pl.pallas_call(
        assemble_units_kernel,
        out_shape=[jax.ShapeDtypeStruct((rows, units), jnp.float32)] * 3,
        grid_spec=pltpu.PrefetchScalarGridSpec(
            num_scalar_prefetch=1,
            grid=(8,),
            in_specs=[spec] * 2,
            out_specs=[pl.BlockSpec((rows, block), lambda r, table: (0, r))] * 3,
        ),
        compiler_params=pltpu.CompilerParams(vmem_limit_bytes=32 * 2**20),
    )(table, mine, other)


def assemble_attn_kernel(table_ref, mine_ref, other_ref, query_ref, out_ref, pair_ref):
    for slot in range(8):
        held = mine_ref if slot < 4 else other_ref
        piece = table_ref[slot]
        cols = pl.ds(pl.multiple_of(piece * LANES, LANES), LANES)
        block = held[slot % 4].astype(jnp.float32)
        query_ref[:, cols] = block[:, :LANES]
        out_ref[:, cols] = block[:, LANES : 2 * LANES]

        @pl.when(piece < 4)
        def _():
            pair_ref[:, cols] = block[:, 2 * LANES :]


def assemble_attn(mine, other):
    rows = mine.shape[1]
    return pl.pallas_call(
        assemble_attn_kernel,
        out_shape=[
            jax.ShapeDtypeStruct((rows, width * LANES), jnp.float32) for width in (8, 8, 4)
        ],
        in_specs=[pl.BlockSpec(memory_space=pltpu.SMEM)]
        + [pl.BlockSpec(memory_space=pltpu.VMEM)] * 2,
        out_specs=[pl.BlockSpec(memory_space=pltpu.VMEM)] * 3,
        compiler_params=pltpu.CompilerParams(vmem_limit_bytes=32 * 2**20),
    )(piece_table(), mine, other)


def to_slots(grad):
    return jnp.transpose(grad.reshape(grad.shape[0], -1, LANES), (1, 0, 2))


def unit_slots(*grads):
    return jnp.concatenate([to_slots(g) for g in grads], axis=2)


def unit_halves(mine, other):
    return plus(mine, swapped(other, "core"))


def unit_blocks(part):
    return exchanged(part.reshape(8, 144, 3 * LANES), GROUP)


def unit_grads(blocks, units):
    mine = jnp.stack(blocks)
    return assemble_units(mine, swapped(mine, "core"), units)


def attn_halves(*grads):
    slots = jnp.concatenate([to_slots(g) for g in grads], axis=2)
    halves = slots.reshape((2, 4) + slots.shape[1:])
    core = lax.axis_index("core")
    return plus(pick(halves, core), swapped(pick(halves, 1 - core), "core"))


def attn_total(blocks):
    total = summed(blocks)
    return plus(total, swapped(total, "yl"))


def attn_grads_of(total):
    mine = jnp.stack(gathered_z(total))
    return assemble_attn(mine, swapped(mine, "core"))


def along(vector, axis):
    if lax.axis_size(axis) == 2:
        return vector + swapped(vector, axis)
    for flip in (1, 2):
        vector = vector + lax.ppermute(vector, axis, [(i, i ^ flip) for i in range(4)])
    return vector


def norm_rows(entries, gain_row):
    return (
        entries
        * lax.rsqrt(jnp.mean(entries * entries, axis=-1, keepdims=True) + EPSILON)
        * gain_row
    )


def turn_tables(position_rows, head_width):
    half_width = head_width // 2
    frequency = ROPE_BASE ** (-2.0 * jnp.arange(half_width, dtype=jnp.float32) / head_width)
    angles = position_rows.astype(jnp.float32)[..., None] * frequency
    return (jnp.cos(angles), jnp.sin(angles))


def rotate(entries, cosine_table, sine_table):
    half_width = entries.shape[-1] // 2
    leading = entries[..., :half_width]
    trailing = entries[..., half_width:]
    return jnp.concatenate(
        [
            leading * cosine_table - trailing * sine_table,
            trailing * cosine_table + leading * sine_table,
        ],
        axis=-1,
    )


def query_piece(raw_proj, gain_row, cosine_table, sine_table):
    head_width = gain_row.shape[0]
    shaped = raw_proj.reshape(cosine_table.shape[0], cosine_table.shape[1], -1, head_width)
    turned = rotate(
        norm_rows(shaped, gain_row), cosine_table[:, :, None, :], sine_table[:, :, None, :]
    )
    return jnp.transpose(turned, (0, 2, 1, 3)) * head_width ** (-0.5)


def key_piece(raw_proj, gain_row, cosine_table, sine_table):
    shaped = raw_proj.reshape(cosine_table.shape[0], cosine_table.shape[1], gain_row.shape[0])
    return rotate(norm_rows(shaped, gain_row), cosine_table, sine_table)


def gelu_product(gate_proj, up_proj):
    return jax.nn.gelu(gate_proj, approximate=True) * up_proj


def masked_scores(queries, key_rows, allowed):
    plain = jnp.einsum("shqd,skd->shqk", queries, key_rows, preferred_element_type=jnp.float32)
    return jnp.where(allowed, plain, MASKED)


def transposed_product(left_side, right_side):
    return lax.dot_general(left_side, right_side, CONTRACT_ROWS, preferred_element_type=jnp.float32)


def product_by_rows(left_side, right_side):
    return lax.dot_general(left_side, right_side, CONTRACT_COLS, preferred_element_type=jnp.float32)


def local(
    tokens,
    positions,
    cotangent,
    gain_attn,
    gain_query,
    gain_key,
    gain_post_attn,
    gain_ffn,
    gain_post_ffn,
    w_query,
    w_key,
    w_value,
    w_out,
    w_gate,
    w_up,
    w_down,
):
    seq_count, tok_rows, model_width = tokens.shape
    all_rows = seq_count * tok_rows
    head_width = gain_query.shape[0]
    query_cols = w_query.shape[1]
    reach_back = min(-(-(WINDOW - 1) // tok_rows), 7)
    cosine_table, sine_table = turn_tables(positions, head_width)
    inputs = tokens.astype(jnp.float32).reshape(all_rows, model_width)
    normed_full, norm_attn_back = jax.vjp(norm_rows, inputs, gain_attn)
    normed = normed_full.astype(jnp.bfloat16)
    qkv_held = by_core(
        w_query[:, :768], jnp.concatenate([w_query[:, 768:], w_key, w_value], axis=1)
    )
    unit_held = unit_pieces(w_gate, w_up, w_down)
    qkv_mine = gathered(qkv_held, GROUP, 8).reshape(model_width, -1)
    qkv_other = swapped(qkv_mine, "core")
    out_held = by_core(w_out[:, :512], w_out[:, 512:])
    unit_stack = exchanged(after(unit_held, qkv_mine), GROUP).reshape(model_width, -1)
    first_raw, second_raw = both_cores(
        jnp.dot(normed, qkv_mine, preferred_element_type=jnp.float32),
        jnp.dot(normed, qkv_other, preferred_element_type=jnp.float32),
    )
    query_raw = jnp.concatenate([first_raw, second_raw[:, :256]], axis=1)
    key_raw = second_raw[:, 256:512]
    value_raw = second_raw[:, 512:]

    def query_local(raw_proj, gain_row):
        return query_piece(raw_proj, gain_row, cosine_table, sine_table)

    def key_local(raw_proj, gain_row):
        return key_piece(raw_proj, gain_row, cosine_table, sine_table)

    queries_full, query_back = jax.vjp(query_local, query_raw, gain_query)
    keys_full, key_back = jax.vjp(key_local, key_raw, gain_key)
    queries = queries_full.astype(jnp.bfloat16)
    local_pairs = jnp.concatenate(
        [keys_full, value_raw.reshape(seq_count, tok_rows, head_width)], axis=-1
    ).astype(jnp.bfloat16)
    out_mine = gathered(after(out_held, (unit_stack, local_pairs)), GROUP, 8)
    out_mine = out_mine.reshape(model_width, -1)
    out_other = swapped(out_mine, "core")
    collected = [local_pairs]
    for distance in range(1, reach_back + 1):
        collected.insert(0, from_behind(local_pairs, distance))
    pair_rows = jnp.concatenate(collected, axis=1)
    key_rows = pair_rows[..., :head_width]
    value_rows = pair_rows[..., head_width:]
    place_index = group_index()
    query_index = place_index * tok_rows + jnp.arange(tok_rows, dtype=jnp.int32)
    key_index = (place_index - reach_back) * tok_rows + jnp.arange(
        (reach_back + 1) * tok_rows, dtype=jnp.int32
    )
    offsets = query_index[:, None] - key_index[None, :]
    doc_start = query_index[None, :] - positions
    allowed = ((offsets >= 0) & (offsets < WINDOW))[None, :, :] & (
        key_index[None, None, :] >= doc_start[:, :, None]
    )
    allowed = allowed[:, None, :, :]
    scores = masked_scores(queries, key_rows, allowed)
    highest = jnp.max(scores, axis=-1, keepdims=True)
    exp_scores = jnp.exp(scores - highest)
    sum_scores = jnp.sum(exp_scores, axis=-1, keepdims=True)
    log_total = highest + jnp.log(sum_scores)
    weights = (exp_scores / sum_scores).astype(jnp.bfloat16)
    mixed_heads = jnp.einsum(
        "shqk,skd->sqhd", weights, value_rows, preferred_element_type=jnp.float32
    )
    attended = mixed_heads.reshape(all_rows, query_cols).astype(jnp.bfloat16)
    unit_blocks_z = gathered_z(after(unit_stack, pair_rows))
    attended_mine, attended_other = both_cores(attended[:, :512], attended[:, 512:])
    attn_branch = product_by_rows(attended_mine, out_mine) + product_by_rows(
        attended_other, out_other
    )
    attn_normed, norm_post_attn_back = jax.vjp(norm_rows, attn_branch, gain_post_attn)
    middle = inputs + attn_normed
    ffn_in_full, norm_ffn_back = jax.vjp(norm_rows, middle, gain_ffn)
    normed_ffn = ffn_in_full.astype(jnp.bfloat16)
    ffn_rows, ffn_block = gather_tokens(normed_ffn)
    gate_cols, up_cols, down_cols = unit_shards(after(unit_blocks_z, ffn_block))
    gate_proj = jnp.dot(ffn_rows, gate_cols, preferred_element_type=jnp.float32)
    up_proj = jnp.dot(ffn_rows, up_cols, preferred_element_type=jnp.float32)
    hidden_full, gelu_back = jax.vjp(gelu_product, gate_proj, up_proj)
    hidden = hidden_full.astype(jnp.bfloat16)
    ffn_branch = scatter_tokens(product_by_rows(hidden, down_cols))
    ffn_normed, norm_post_ffn_back = jax.vjp(norm_rows, ffn_branch, gain_post_ffn)
    outputs = (middle + ffn_normed).astype(jnp.bfloat16).reshape(seq_count, tok_rows, model_width)
    upstream = cotangent.astype(jnp.float32).reshape(all_rows, model_width)
    grad_ffn_branch, grad_post_ffn = norm_post_ffn_back(upstream)
    grad_ffn_branch = grad_ffn_branch.astype(jnp.bfloat16)
    grad_branch_rows, _ = gather_tokens(grad_ffn_branch)
    grad_hidden = jnp.dot(grad_branch_rows, down_cols, preferred_element_type=jnp.float32)
    grad_gate_full, grad_up_full = gelu_back(grad_hidden)
    grad_gate_part = grad_gate_full.astype(jnp.bfloat16)
    grad_up_part = grad_up_full.astype(jnp.bfloat16)
    grad_partial = product_by_rows(grad_gate_part, gate_cols) + product_by_rows(
        grad_up_part, up_cols
    )
    grad_normed_ffn = scatter_tokens(grad_partial)
    ffn_rows, grad_branch_rows, _ = lax.optimization_barrier(
        (ffn_rows, grad_branch_rows, grad_normed_ffn)
    )
    unit_pairs = (
        (ffn_rows, grad_gate_part),
        (ffn_rows, grad_up_part),
        (grad_branch_rows, hidden),
    )
    own_slots, other_slots = [
        unit_slots(
            *[transposed_product(rows, units[:, cols]).astype(jnp.bfloat16) for rows, units in unit_pairs]
        )
        for cols in (slice(0, 4 * LANES), slice(4 * LANES, 8 * LANES))
    ]
    own_halves = unit_halves(own_slots, other_slots)
    own_part = summed(exchanged(own_halves, "z"))
    grad_middle_part, grad_gain_ffn = norm_ffn_back(grad_normed_ffn)
    grad_middle = upstream + grad_middle_part
    grad_attn_branch, grad_post_attn = norm_post_attn_back(grad_middle)
    grad_attn_branch = after(grad_attn_branch.astype(jnp.bfloat16), own_halves)
    out_halves = attn_halves(
        transposed_product(grad_attn_branch, attended).astype(jnp.bfloat16)
    )
    grad_attended = jnp.concatenate(
        both_cores(
            jnp.dot(grad_attn_branch, out_mine, preferred_element_type=jnp.float32),
            jnp.dot(grad_attn_branch, out_other, preferred_element_type=jnp.float32),
        ),
        axis=1,
    )
    grad_heads = grad_attended.astype(jnp.bfloat16).reshape(seq_count, tok_rows, HEADS, head_width)
    scores = masked_scores(queries, key_rows, allowed)
    probabilities = jnp.exp(scores - log_total)
    grad_probs = jnp.einsum(
        "sqhd,skd->shqk", grad_heads, value_rows, preferred_element_type=jnp.float32
    )
    centre = jnp.sum(probabilities * grad_probs, axis=-1, keepdims=True)
    grad_scores = (probabilities * (grad_probs - centre)).astype(jnp.bfloat16)
    grad_queries = jnp.einsum(
        "shqk,skd->shqd", grad_scores, key_rows, preferred_element_type=jnp.float32
    )
    grad_key_rows = jnp.einsum(
        "shqk,shqd->skd", grad_scores, queries, preferred_element_type=jnp.float32
    )
    grad_value_rows = jnp.einsum(
        "shqk,sqhd->skd",
        probabilities.astype(jnp.bfloat16),
        grad_heads,
        preferred_element_type=jnp.float32,
    )
    grad_pairs = jnp.concatenate([grad_key_rows, grad_value_rows], axis=-1)
    own_blocks = unit_blocks(after(own_part, grad_pairs))
    own_pairs = grad_pairs[:, reach_back * tok_rows :]
    for distance in range(1, reach_back + 1):
        lower_block = reach_back - distance
        sent_block = grad_pairs[:, lower_block * tok_rows : (lower_block + 1) * tok_rows]
        own_pairs = own_pairs + from_behind(
            sent_block.astype(jnp.bfloat16), -distance
        ).astype(sent_block.dtype)
    grad_key_raw, grad_gain_key = key_back(own_pairs[..., :head_width])
    grad_query_raw, grad_gain_query = query_back(grad_queries)
    grad_value_raw = own_pairs[..., head_width:].reshape(all_rows, head_width)
    grad_projected = jnp.concatenate([grad_query_raw, grad_key_raw, grad_value_raw], axis=1).astype(
        jnp.bfloat16
    )
    late_projected = after(grad_projected, own_blocks)
    projected_mine, projected_other = both_cores(late_projected[:, :768], late_projected[:, 768:])
    contribution = product_by_rows(projected_mine, qkv_mine) + product_by_rows(
        projected_other, qkv_other
    )
    projected_part = transposed_product(normed, after(grad_projected, own_part)).astype(
        jnp.bfloat16
    )
    qkv_halves = attn_halves(
        projected_part[:, :query_cols],
        jnp.pad(projected_part[:, query_cols:], ((0, 0), (0, 512))),
    )
    grad_inputs_part, grad_gain_attn = norm_attn_back(contribution)
    grad_tokens = (grad_middle + grad_inputs_part).reshape(seq_count, tok_rows, model_width)
    gains = along(
        jnp.concatenate(
            [
                grad_gain_attn,
                grad_gain_query,
                grad_gain_key,
                grad_post_attn,
                grad_gain_ffn,
                grad_post_ffn,
            ]
        ),
        "z",
    )
    attn_pieces = jnp.concatenate(
        [qkv_halves[..., :LANES], out_halves, qkv_halves[..., LANES:]], axis=2
    )
    attn_pieces = exchanged(after(attn_pieces, (own_blocks, gains)), "z")
    for axis in ("core", "yl", "x", "yh"):
        gains = along(gains, axis)
    attn_pieces = after(attn_pieces, gains)
    attn_blocks = exchanged(summed(attn_pieces).reshape(8, 144, 3 * LANES), GROUP)
    own_blocks = plus(own_blocks, swapped(own_blocks, "yl"))
    attn_sum = attn_total(attn_blocks)
    own_gathered = gathered_z(after(own_blocks, attn_pieces))
    grad_gate_total, grad_up_total, grad_down_total = unit_grads(
        after(own_gathered, attn_sum), w_gate.shape[1]
    )
    query_total, grad_out_total, pair_total = attn_grads_of(attn_sum)
    query_at, key_at = model_width, model_width + head_width
    wide_at = key_at + head_width
    return (
        outputs,
        grad_tokens,
        gains[:query_at],
        gains[query_at:key_at],
        gains[key_at:wide_at],
        gains[wide_at : wide_at + model_width],
        gains[wide_at + model_width : wide_at + 2 * model_width],
        gains[wide_at + 2 * model_width :],
        query_total,
        pair_total[:, :head_width],
        pair_total[:, head_width:],
        grad_out_total,
        grad_gate_total,
        grad_up_total,
        grad_down_total,
    )


def solution(mesh):
    fine = Mesh(mesh.devices.reshape(4, 2, 4, 2, 2), GROUP + REPLICA)
    placed = (
        P(REPLICA, GROUP, None),
        P(REPLICA, GROUP),
        P(REPLICA, GROUP, None),
        P(),
        P(),
        P(),
        P(),
        P(),
        P(),
        P(GROUP, None),
        P(GROUP, None),
        P(GROUP, None),
        P(GROUP, None),
        P(GROUP, None),
        P(GROUP, None),
        P(GROUP, None),
    )
    return jax.shard_map(
        local,
        mesh=fine,
        in_specs=placed,
        out_specs=(
            P(REPLICA, GROUP, None),
            P(REPLICA, GROUP, None),
            P(),
            P(),
            P(),
            P(),
            P(),
            P(),
            P(GROUP, None),
            P(GROUP, None),
            P(GROUP, None),
            P(GROUP, None),
            P(GROUP, None),
            P(GROUP, None),
            P(GROUP, None),
        ),
        check_vma=False,
    )
```

```python
import jax
import jax.numpy as jnp
from jax import lax
from jax.experimental import pallas as pl
from jax.experimental.pallas import tpu as pltpu
from jax.sharding import Mesh
from jax.sharding import PartitionSpec as P

HEADS = 4
WINDOW = 512


EPSILON = 1e-06
ROPE_BASE = 10000.0
MASKED = -1e30
CONTRACT_COLS = (((1,), (1,)), ((), ()))
CONTRACT_ROWS = (((0,), (0,)), ((), ()))


GROUP = ("x", "yh")
REPLICA = ("z", "yl", "core")
SHIFTS = ((1, 0), (3, 0), (0, 1), (1, 1), (3, 1), (2, 0), (2, 1))
Z_STEPS = (1, 3, 2)
LANES = 128
UNIT_TILES = 7


def from_behind(block, distance):
    devices = range(8)
    route = [(i - distance, i) for i in devices if i - distance in devices]
    return lax.ppermute(block, GROUP, route)


def shifted(block, step):
    route = [(a * 2 + b, (a + step[0]) % 4 * 2 + (b ^ step[1])) for a in range(4) for b in range(2)]
    return lax.ppermute(block, GROUP, route)


def turned(block, axis, step, size):
    return lax.ppermute(block, axis, [(i, (i + step) % size) for i in range(size)])


def swapped(block, axis):
    return turned(block, axis, 1, 2)


def pick(stack, index):
    return lax.dynamic_index_in_dim(stack, index, 0, keepdims=False)


def place(stack, block, index):
    return lax.dynamic_update_index_in_dim(stack, block, index, 0)


def along_z():
    depth = lax.axis_index("z")
    return [lax.rem(depth + 4 - step, 4) for step in (0,) + Z_STEPS]


def gathered_z(block):
    return [block] + [turned(block, "z", step, 4) for step in Z_STEPS]


def after(value, other):
    return lax.optimization_barrier((value, other))[0]


def group_index():
    return lax.axis_index("x") * 2 + lax.axis_index("yh")


def exchanged(stack, axes):
    return lax.all_to_all(stack, axes, 0, 0)


def gathered(block, axes, size):
    return exchanged(jnp.broadcast_to(block, (size,) + block.shape), axes)


def on_first_core():
    return lax.axis_index("core") == 0


def by_core(first, second):
    return jnp.where(on_first_core(), first, second)


def both_cores(mine, other):
    return by_core(mine, other), by_core(other, mine)


def gather_tokens(rows):
    blocks = [rows] + [shifted(rows, step) for step in SHIFTS]
    return jnp.concatenate(blocks, axis=0), blocks[1]


def scatter_tokens(partial):
    rows = partial.shape[0] // 8
    total = partial[:rows]
    blocks = []
    for i, step in enumerate(SHIFTS):
        back = ((4 - step[0]) % 4, step[1])
        block = partial[(i + 1) * rows : (i + 2) * rows].astype(jnp.bfloat16)
        blocks.append(shifted(block, back))
    for block in blocks:
        total = total + block.astype(jnp.float32)
    return total


def piece_table():
    core = lax.axis_index("core")
    return jnp.stack([half * 4 + z for half in (core, 1 - core) for z in along_z()])


def unit_kernel(piece_ref, gate_ref, up_ref, down_ref, out_ref):
    piece = piece_ref[0]
    real = (piece < UNIT_TILES) & (pl.program_id(0) * UNIT_TILES + piece < piece_ref[1])
    for i, ref in enumerate((gate_ref, up_ref, down_ref)):
        block = ref[...]
        out_ref[0, :, i * LANES : (i + 1) * LANES] = jnp.where(real, block, jnp.zeros_like(block))


def unit_pieces(w_gate, w_up, w_down):
    rows, units = w_gate.shape
    tiles = units // LANES
    piece = lax.axis_index("core") * 4 + lax.axis_index("z")
    numbers = jnp.stack([piece, jnp.int32(tiles)])
    spec = pl.BlockSpec(
        (rows, LANES), lambda j, num: (0, jnp.minimum(j * UNIT_TILES + num[0], tiles - 1))
    )
    return pl.pallas_call(
        unit_kernel,
        out_shape=jax.ShapeDtypeStruct((8, rows, 3 * LANES), jnp.bfloat16),
        grid_spec=pltpu.PrefetchScalarGridSpec(
            num_scalar_prefetch=1,
            grid=(8,),
            in_specs=[spec] * 3,
            out_specs=pl.BlockSpec((1, rows, 3 * LANES), lambda j, num: (j, 0, 0)),
        ),
    )(numbers, w_gate, w_up, w_down)


def unit_shards(blocks):
    mine = jnp.zeros((4,) + blocks[0].shape, blocks[0].dtype)
    for block, z in zip(blocks, along_z()):
        mine = place(mine, block, z)
    other = swapped(mine, "core")
    slots = [mine[i] for i in range(4)] + [other[i] for i in range(4)]
    return tuple(
        jnp.concatenate([slot[:, i * LANES : (i + 1) * LANES] for slot in slots], axis=1)
        for i in range(3)
    )


def plus(*blocks):
    return sum(block.astype(jnp.float32) for block in blocks).astype(jnp.bfloat16)


def summed(stack):
    return jnp.sum(stack.astype(jnp.float32), axis=0).astype(jnp.bfloat16)


def assemble_units_kernel(table_ref, mine_ref, other_ref, *out_refs):
    for slot in range(8):
        held = mine_ref if slot < 4 else other_ref
        piece = table_ref[slot]

        @pl.when(piece < UNIT_TILES)
        def _():
            cols = pl.ds(pl.multiple_of(piece * LANES, LANES), LANES)
            for i, out_ref in enumerate(out_refs):
                block = held[slot % 4, 0, :, i * LANES : (i + 1) * LANES]
                out_ref[:, cols] = block.astype(jnp.float32)


def assemble_units(mine, other, units):
    rows = mine.shape[2]
    table = piece_table()
    block = UNIT_TILES * LANES
    spec = pl.BlockSpec((4, 1, rows, 3 * LANES), lambda r, table: (0, r, 0, 0))
    return pl.pallas_call(
        assemble_units_kernel,
        out_shape=[jax.ShapeDtypeStruct((rows, units), jnp.float32)] * 3,
        grid_spec=pltpu.PrefetchScalarGridSpec(
            num_scalar_prefetch=1,
            grid=(8,),
            in_specs=[spec] * 2,
            out_specs=[pl.BlockSpec((rows, block), lambda r, table: (0, r))] * 3,
        ),
        compiler_params=pltpu.CompilerParams(vmem_limit_bytes=32 * 2**20),
    )(table, mine, other)


def assemble_attn_kernel(table_ref, mine_ref, other_ref, query_ref, out_ref, pair_ref):
    for slot in range(8):
        held = mine_ref if slot < 4 else other_ref
        piece = table_ref[slot]
        cols = pl.ds(pl.multiple_of(piece * LANES, LANES), LANES)
        block = held[slot % 4].astype(jnp.float32)
        query_ref[:, cols] = block[:, :LANES]
        out_ref[:, cols] = block[:, LANES : 2 * LANES]

        @pl.when(piece < 4)
        def _():
            pair_ref[:, cols] = block[:, 2 * LANES :]


def assemble_attn(mine, other):
    rows = mine.shape[1]
    return pl.pallas_call(
        assemble_attn_kernel,
        out_shape=[
            jax.ShapeDtypeStruct((rows, width * LANES), jnp.float32) for width in (8, 8, 4)
        ],
        in_specs=[pl.BlockSpec(memory_space=pltpu.SMEM)]
        + [pl.BlockSpec(memory_space=pltpu.VMEM)] * 2,
        out_specs=[pl.BlockSpec(memory_space=pltpu.VMEM)] * 3,
        compiler_params=pltpu.CompilerParams(vmem_limit_bytes=32 * 2**20),
    )(piece_table(), mine, other)


def to_slots(grad):
    return jnp.transpose(grad.reshape(grad.shape[0], -1, LANES), (1, 0, 2))


def unit_slots(*grads):
    return jnp.concatenate([to_slots(g) for g in grads], axis=2)


def unit_halves(mine, other):
    return plus(mine, swapped(other, "core"))


def unit_blocks(part):
    return exchanged(part.reshape(8, 144, 3 * LANES), GROUP)


def unit_grads(blocks, units):
    mine = jnp.stack(blocks)
    return assemble_units(mine, swapped(mine, "core"), units)


def attn_halves(*grads):
    slots = jnp.concatenate([to_slots(g) for g in grads], axis=2)
    halves = slots.reshape((2, 4) + slots.shape[1:])
    core = lax.axis_index("core")
    return plus(pick(halves, core), swapped(pick(halves, 1 - core), "core"))


def attn_total(blocks):
    total = summed(blocks)
    return plus(total, swapped(total, "yl"))


def attn_grads_of(total):
    mine = jnp.stack(gathered_z(total))
    return assemble_attn(mine, swapped(mine, "core"))


def along(vector, axis):
    if lax.axis_size(axis) == 2:
        return vector + swapped(vector, axis)
    for flip in (1, 2):
        vector = vector + lax.ppermute(vector, axis, [(i, i ^ flip) for i in range(4)])
    return vector


def norm_rows(entries, gain_row):
    return (
        entries
        * lax.rsqrt(jnp.mean(entries * entries, axis=-1, keepdims=True) + EPSILON)
        * gain_row
    )


def turn_tables(position_rows, head_width):
    half_width = head_width // 2
    frequency = ROPE_BASE ** (-2.0 * jnp.arange(half_width, dtype=jnp.float32) / head_width)
    angles = position_rows.astype(jnp.float32)[..., None] * frequency
    return (jnp.cos(angles), jnp.sin(angles))


def rotate(entries, cosine_table, sine_table):
    half_width = entries.shape[-1] // 2
    leading = entries[..., :half_width]
    trailing = entries[..., half_width:]
    return jnp.concatenate(
        [
            leading * cosine_table - trailing * sine_table,
            trailing * cosine_table + leading * sine_table,
        ],
        axis=-1,
    )


def query_piece(raw_proj, gain_row, cosine_table, sine_table):
    head_width = gain_row.shape[0]
    shaped = raw_proj.reshape(cosine_table.shape[0], cosine_table.shape[1], -1, head_width)
    turned = rotate(
        norm_rows(shaped, gain_row), cosine_table[:, :, None, :], sine_table[:, :, None, :]
    )
    return jnp.transpose(turned, (0, 2, 1, 3)) * head_width ** (-0.5)


def key_piece(raw_proj, gain_row, cosine_table, sine_table):
    shaped = raw_proj.reshape(cosine_table.shape[0], cosine_table.shape[1], gain_row.shape[0])
    return rotate(norm_rows(shaped, gain_row), cosine_table, sine_table)


def gelu_product(gate_proj, up_proj):
    return jax.nn.gelu(gate_proj, approximate=True) * up_proj


def masked_scores(queries, key_rows, allowed):
    plain = jnp.einsum("shqd,skd->shqk", queries, key_rows, preferred_element_type=jnp.float32)
    return jnp.where(allowed, plain, MASKED)


def transposed_product(left_side, right_side):
    return lax.dot_general(left_side, right_side, CONTRACT_ROWS, preferred_element_type=jnp.float32)


def product_by_rows(left_side, right_side):
    return lax.dot_general(left_side, right_side, CONTRACT_COLS, preferred_element_type=jnp.float32)


def local(
    tokens,
    positions,
    cotangent,
    gain_attn,
    gain_query,
    gain_key,
    gain_post_attn,
    gain_ffn,
    gain_post_ffn,
    w_query,
    w_key,
    w_value,
    w_out,
    w_gate,
    w_up,
    w_down,
):
    seq_count, tok_rows, model_width = tokens.shape
    all_rows = seq_count * tok_rows
    head_width = gain_query.shape[0]
    query_cols = w_query.shape[1]
    reach_back = min(-(-(WINDOW - 1) // tok_rows), 7)
    cosine_table, sine_table = turn_tables(positions, head_width)
    inputs = tokens.astype(jnp.float32).reshape(all_rows, model_width)
    normed_full, norm_attn_back = jax.vjp(norm_rows, inputs, gain_attn)
    normed = normed_full.astype(jnp.bfloat16)
    qkv_held = by_core(
        w_query[:, :768], jnp.concatenate([w_query[:, 768:], w_key, w_value], axis=1)
    )
    unit_held = unit_pieces(w_gate, w_up, w_down)
    qkv_mine = gathered(qkv_held, GROUP, 8).reshape(model_width, -1)
    qkv_other = swapped(qkv_mine, "core")
    out_held = by_core(w_out[:, :512], w_out[:, 512:])
    unit_stack = exchanged(after(unit_held, qkv_mine), GROUP).reshape(model_width, -1)
    first_raw, second_raw = both_cores(
        jnp.dot(normed, qkv_mine, preferred_element_type=jnp.float32),
        jnp.dot(normed, qkv_other, preferred_element_type=jnp.float32),
    )
    query_raw = jnp.concatenate([first_raw, second_raw[:, :256]], axis=1)
    key_raw = second_raw[:, 256:512]
    value_raw = second_raw[:, 512:]

    def query_local(raw_proj, gain_row):
        return query_piece(raw_proj, gain_row, cosine_table, sine_table)

    def key_local(raw_proj, gain_row):
        return key_piece(raw_proj, gain_row, cosine_table, sine_table)

    queries_full, query_back = jax.vjp(query_local, query_raw, gain_query)
    keys_full, key_back = jax.vjp(key_local, key_raw, gain_key)
    queries = queries_full.astype(jnp.bfloat16)
    local_pairs = jnp.concatenate(
        [keys_full, value_raw.reshape(seq_count, tok_rows, head_width)], axis=-1
    ).astype(jnp.bfloat16)
    out_mine = gathered(after(out_held, (unit_stack, local_pairs)), GROUP, 8)
    out_mine = out_mine.reshape(model_width, -1)
    out_other = swapped(out_mine, "core")
    collected = [local_pairs]
    for distance in range(1, reach_back + 1):
        collected.insert(0, from_behind(local_pairs, distance))
    pair_rows = jnp.concatenate(collected, axis=1)
    key_rows = pair_rows[..., :head_width]
    value_rows = pair_rows[..., head_width:]
    place_index = group_index()
    query_index = place_index * tok_rows + jnp.arange(tok_rows, dtype=jnp.int32)
    key_index = (place_index - reach_back) * tok_rows + jnp.arange(
        (reach_back + 1) * tok_rows, dtype=jnp.int32
    )
    offsets = query_index[:, None] - key_index[None, :]
    doc_start = query_index[None, :] - positions
    allowed = ((offsets >= 0) & (offsets < WINDOW))[None, :, :] & (
        key_index[None, None, :] >= doc_start[:, :, None]
    )
    allowed = allowed[:, None, :, :]
    scores = masked_scores(queries, key_rows, allowed)
    highest = jnp.max(scores, axis=-1, keepdims=True)
    exp_scores = jnp.exp(scores - highest)
    sum_scores = jnp.sum(exp_scores, axis=-1, keepdims=True)
    log_total = highest + jnp.log(sum_scores)
    weights = (exp_scores / sum_scores).astype(jnp.bfloat16)
    mixed_heads = jnp.einsum(
        "shqk,skd->sqhd", weights, value_rows, preferred_element_type=jnp.float32
    )
    attended = mixed_heads.reshape(all_rows, query_cols).astype(jnp.bfloat16)
    unit_blocks_z = gathered_z(after(unit_stack, pair_rows))
    attended_mine, attended_other = both_cores(attended[:, :512], attended[:, 512:])
    attn_branch = product_by_rows(attended_mine, out_mine) + product_by_rows(
        attended_other, out_other
    )
    attn_normed, norm_post_attn_back = jax.vjp(norm_rows, attn_branch, gain_post_attn)
    middle = inputs + attn_normed
    ffn_in_full, norm_ffn_back = jax.vjp(norm_rows, middle, gain_ffn)
    normed_ffn = ffn_in_full.astype(jnp.bfloat16)
    ffn_rows, ffn_block = gather_tokens(normed_ffn)
    gate_cols, up_cols, down_cols = unit_shards(after(unit_blocks_z, ffn_block))
    gate_proj = jnp.dot(ffn_rows, gate_cols, preferred_element_type=jnp.float32)
    up_proj = jnp.dot(ffn_rows, up_cols, preferred_element_type=jnp.float32)
    hidden_full, gelu_back = jax.vjp(gelu_product, gate_proj, up_proj)
    hidden = hidden_full.astype(jnp.bfloat16)
    ffn_branch = scatter_tokens(product_by_rows(hidden, down_cols))
    ffn_normed, norm_post_ffn_back = jax.vjp(norm_rows, ffn_branch, gain_post_ffn)
    outputs = (middle + ffn_normed).astype(jnp.bfloat16).reshape(seq_count, tok_rows, model_width)
    upstream = cotangent.astype(jnp.float32).reshape(all_rows, model_width)
    grad_ffn_branch, grad_post_ffn = norm_post_ffn_back(upstream)
    grad_ffn_branch = grad_ffn_branch.astype(jnp.bfloat16)
    grad_branch_rows, _ = gather_tokens(grad_ffn_branch)
    grad_hidden = jnp.dot(grad_branch_rows, down_cols, preferred_element_type=jnp.float32)
    grad_gate_full, grad_up_full = gelu_back(grad_hidden)
    grad_gate_part = grad_gate_full.astype(jnp.bfloat16)
    grad_up_part = grad_up_full.astype(jnp.bfloat16)
    grad_partial = product_by_rows(grad_gate_part, gate_cols) + product_by_rows(
        grad_up_part, up_cols
    )
    grad_normed_ffn = scatter_tokens(grad_partial)
    ffn_rows, grad_branch_rows, _ = lax.optimization_barrier(
        (ffn_rows, grad_branch_rows, grad_normed_ffn)
    )
    unit_pairs = (
        (ffn_rows, grad_gate_part),
        (ffn_rows, grad_up_part),
        (grad_branch_rows, hidden),
    )
    own_slots, other_slots = [
        unit_slots(
            *[transposed_product(rows, units[:, cols]).astype(jnp.bfloat16) for rows, units in unit_pairs]
        )
        for cols in (slice(0, 4 * LANES), slice(4 * LANES, 8 * LANES))
    ]
    own_halves = unit_halves(own_slots, other_slots)
    own_part = summed(exchanged(own_halves, "z"))
    grad_middle_part, grad_gain_ffn = norm_ffn_back(grad_normed_ffn)
    grad_middle = upstream + grad_middle_part
    grad_attn_branch, grad_post_attn = norm_post_attn_back(grad_middle)
    grad_attn_branch = after(grad_attn_branch.astype(jnp.bfloat16), own_halves)
    out_halves = attn_halves(
        transposed_product(grad_attn_branch, attended).astype(jnp.bfloat16)
    )
    grad_attended = jnp.concatenate(
        both_cores(
            jnp.dot(grad_attn_branch, out_mine, preferred_element_type=jnp.float32),
            jnp.dot(grad_attn_branch, out_other, preferred_element_type=jnp.float32),
        ),
        axis=1,
    )
    grad_heads = grad_attended.astype(jnp.bfloat16).reshape(seq_count, tok_rows, HEADS, head_width)
    scores = masked_scores(queries, key_rows, allowed)
    probabilities = jnp.exp(scores - log_total)
    grad_probs = jnp.einsum(
        "sqhd,skd->shqk", grad_heads, value_rows, preferred_element_type=jnp.float32
    )
    centre = jnp.sum(probabilities * grad_probs, axis=-1, keepdims=True)
    grad_scores = (probabilities * (grad_probs - centre)).astype(jnp.bfloat16)
    grad_queries = jnp.einsum(
        "shqk,skd->shqd", grad_scores, key_rows, preferred_element_type=jnp.float32
    )
    grad_key_rows = jnp.einsum(
        "shqk,shqd->skd", grad_scores, queries, preferred_element_type=jnp.float32
    )
    grad_value_rows = jnp.einsum(
        "shqk,sqhd->skd",
        probabilities.astype(jnp.bfloat16),
        grad_heads,
        preferred_element_type=jnp.float32,
    )
    grad_pairs = jnp.concatenate([grad_key_rows, grad_value_rows], axis=-1)
    own_blocks = unit_blocks(after(own_part, grad_pairs))
    own_pairs = grad_pairs[:, reach_back * tok_rows :]
    for distance in range(1, reach_back + 1):
        lower_block = reach_back - distance
        sent_block = grad_pairs[:, lower_block * tok_rows : (lower_block + 1) * tok_rows]
        own_pairs = own_pairs + from_behind(
            sent_block.astype(jnp.bfloat16), -distance
        ).astype(sent_block.dtype)
    grad_key_raw, grad_gain_key = key_back(own_pairs[..., :head_width])
    grad_query_raw, grad_gain_query = query_back(grad_queries)
    grad_value_raw = own_pairs[..., head_width:].reshape(all_rows, head_width)
    grad_projected = jnp.concatenate([grad_query_raw, grad_key_raw, grad_value_raw], axis=1).astype(
        jnp.bfloat16
    )
    late_projected = after(grad_projected, own_blocks)
    projected_mine, projected_other = both_cores(late_projected[:, :768], late_projected[:, 768:])
    contribution = product_by_rows(projected_mine, qkv_mine) + product_by_rows(
        projected_other, qkv_other
    )
    projected_part = transposed_product(normed, after(grad_projected, own_part)).astype(
        jnp.bfloat16
    )
    qkv_halves = attn_halves(
        projected_part[:, :query_cols],
        jnp.pad(projected_part[:, query_cols:], ((0, 0), (0, 512))),
    )
    grad_inputs_part, grad_gain_attn = norm_attn_back(contribution)
    grad_tokens = (grad_middle + grad_inputs_part).reshape(seq_count, tok_rows, model_width)
    gains = along(
        jnp.concatenate(
            [
                grad_gain_attn,
                grad_gain_query,
                grad_gain_key,
                grad_post_attn,
                grad_gain_ffn,
                grad_post_ffn,
            ]
        ),
        "z",
    )
    attn_pieces = jnp.concatenate(
        [qkv_halves[..., :LANES], out_halves, qkv_halves[..., LANES:]], axis=2
    )
    attn_pieces = exchanged(after(attn_pieces, own_blocks), "z")
    for axis in ("core", "yl", "x", "yh"):
        gains = along(gains, axis)
    attn_pieces = after(attn_pieces, gains)
    attn_blocks = exchanged(summed(attn_pieces).reshape(8, 144, 3 * LANES), GROUP)
    own_blocks = plus(own_blocks, swapped(own_blocks, "yl"))
    attn_sum = attn_total(attn_blocks)
    own_gathered = gathered_z(after(own_blocks, attn_pieces))
    grad_gate_total, grad_up_total, grad_down_total = unit_grads(
        after(own_gathered, attn_sum), w_gate.shape[1]
    )
    query_total, grad_out_total, pair_total = attn_grads_of(attn_sum)
    query_at, key_at = model_width, model_width + head_width
    wide_at = key_at + head_width
    return (
        outputs,
        grad_tokens,
        gains[:query_at],
        gains[query_at:key_at],
        gains[key_at:wide_at],
        gains[wide_at : wide_at + model_width],
        gains[wide_at + model_width : wide_at + 2 * model_width],
        gains[wide_at + 2 * model_width :],
        query_total,
        pair_total[:, :head_width],
        pair_total[:, head_width:],
        grad_out_total,
        grad_gate_total,
        grad_up_total,
        grad_down_total,
    )


def solution(mesh):
    fine = Mesh(mesh.devices.reshape(4, 2, 4, 2, 2), GROUP + REPLICA)
    placed = (
        P(REPLICA, GROUP, None),
        P(REPLICA, GROUP),
        P(REPLICA, GROUP, None),
        P(),
        P(),
        P(),
        P(),
        P(),
        P(),
        P(GROUP, None),
        P(GROUP, None),
        P(GROUP, None),
        P(GROUP, None),
        P(GROUP, None),
        P(GROUP, None),
        P(GROUP, None),
    )
    return jax.shard_map(
        local,
        mesh=fine,
        in_specs=placed,
        out_specs=(
            P(REPLICA, GROUP, None),
            P(REPLICA, GROUP, None),
            P(),
            P(),
            P(),
            P(),
            P(),
            P(),
            P(GROUP, None),
            P(GROUP, None),
            P(GROUP, None),
            P(GROUP, None),
            P(GROUP, None),
            P(GROUP, None),
            P(GROUP, None),
        ),
        check_vma=False,
    )
```
